32 devices in a mesh: cuts: 4 (over y, x), layer: 8 (over z, core).
Axes of the slice: x: 2, y: 2, z: 4, core: 2. Of those that a mesh axis runs over, the one named last changes fastest.
Arguments:
- vectors: float32 [4, 64, 16, 1024], P('cuts', None, 'layer'), may hold values from -40 to 40
- diag_blocks: bfloat16 [16, 1024, 1024], P('layer'), may hold values from -1 to 1, as said below
- couplings: bfloat16 [16, 1024, 1024], P('layer'), may hold values from -0.09375 to 0.09375
- bounds: int32 [4, 2], P('cuts'), may hold values from -128 to 160, as said below
Outputs:
- filtered: float32 [4, 64, 16, 1024], P('cuts', None, 'layer')
The draws below stay inside these ranges and needn't reach their ends.
Inputs may be any that keep to these rules, and one draw needn't show every extreme that they name: `bounds`: column 0 holds each slice's lower end, which is -128 at slice 0 and to at most -81; column 1 holds its upper end, from 128 to 160. `diag_blocks`: each block is symmetric.
All inputs are finite; a program needn't handle non-finite values.
Results may differ from the reference program's by a relative error of at most 0.012.
Values may be sent and summed in bfloat16 or wider, within the bound.
No kernel may reach another device: no remote copies, remote signals or barrier semaphores. Data moves between devices by JAX's collectives and lax.ppermute only.
A program may use at most 64 MiB of HBM per device.

```python
import math
import jax
import jax.numpy as jnp
from jax import lax

B = 1024
K = 64
EDGE = 16
DEG = 4
STEPS = 2
SLICES = 4
NL = 16
ORDER = 16384


def draw_bounds(key, part):
    first_key, second_key = jax.random.split(jax.random.fold_in(key, 11))
    slice_index = jnp.arange(SLICES).astype(jnp.int32)
    rising = 40 * slice_index // max(SLICES - 1, 1)
    jitter = jax.random.randint(first_key, (SLICES,), 0, 8) * (slice_index > 0).astype(jnp.int32)
    bottom = -128 + rising + jitter
    summit = jax.random.randint(second_key, (SLICES,), 128, 161)
    return jnp.stack([bottom, summit], 1).astype(jnp.int32)


def draw_diag_blocks(key, part):
    inner_key = jax.random.fold_in(key, 23)
    raw = jax.random.normal(inner_key, (NL, B, B), jnp.float32)
    symmetric = (raw + jnp.swapaxes(raw, 1, 2)) / (2.0 * math.sqrt(B))
    return jnp.clip(symmetric, -1.0, 1.0).astype(jnp.bfloat16)


def draw_vectors(key, part):
    keys = jax.random.split(jax.random.fold_in(key, 37), 3)
    layer_pos = jnp.arange(NL).astype(jnp.float32) / max(NL - 1, 1)
    own = jax.random.normal(keys[0], (SLICES, K, NL, B), jnp.float32)
    shared = jax.random.normal(keys[1], (SLICES, EDGE, NL, B), jnp.float32)
    spread = jnp.exp(jax.random.uniform(keys[2], (NL,), jnp.float32, 0.0, math.log(3.2)))
    rising = jnp.sqrt(1.0 + 2.0 * layer_pos)
    block = 0.6 * own
    block = block.at[:, :EDGE].add(0.8 * jnp.roll(shared, 1, 0))
    block = block.at[:, K - EDGE:].add(0.8 * shared)
    scale = (rising * spread).reshape(1, 1, NL, 1)
    return jnp.clip(block * scale, -40.0, 40.0).astype(jnp.float32)


def block_levels(key, shape, shards, low, high):
    def one(axis_at, shards_of):
        heights = jax.random.uniform(jax.random.fold_in(jax.random.fold_in(key, 6), axis_at), (shards_of,), jnp.float32, low / len(shards), high / len(shards))
        return jnp.repeat(jnp.exp(heights), shape[axis_at] // shards_of).reshape((-1,) + (1,) * (len(shape) - axis_at - 1))

    level = one(*shards[0])
    for cut in shards[1:]:
        level = level * one(*cut)
    return level


def centred(rng, dims, scale, reach, cuts=(), held_as=jnp.bfloat16):
    values = scale * jax.random.normal(rng, dims, jnp.float32)
    if cuts:
        values = values * block_levels(rng, dims, cuts, -0.22, 0.18)
    return jnp.clip(values, -reach, reach).astype(held_as)


def setup_inputs(seed: int = 0) -> dict:
    streams_of = jax.random.split(jax.random.key(seed), 5)
    return {
        "vectors": draw_vectors(jax.random.fold_in(streams_of[4], 71), 0),
        "diag_blocks": draw_diag_blocks(jax.random.fold_in(streams_of[4], 71), 0),
        "couplings": centred(streams_of[2], (NL, B, B), (4 * B) ** -0.5, 0.09375, ((0, 8),)),
        "bounds": draw_bounds(jax.random.fold_in(streams_of[4], 71), 0),
    }


def apply_hamiltonian(vectors_now, blocks_diag, blocks_link):
    rounded = lax.optimization_barrier(vectors_now.astype(jnp.bfloat16)).astype(jnp.float32)
    result = jnp.einsum('skld,lde->skle', rounded, blocks_diag, precision=lax.Precision.HIGHEST)
    upward = jnp.einsum('skle,lde->skld', rounded[:, :, 1:], blocks_link[:-1], precision=lax.Precision.HIGHEST)
    downward = jnp.einsum('skld,lde->skle', rounded[:, :, :-1], blocks_link[:-1], precision=lax.Precision.HIGHEST)
    zero_layer = jnp.zeros_like(rounded[:, :, :1])
    result = result + jnp.concatenate([upward, zero_layer], 2)
    return result + jnp.concatenate([zero_layer, downward], 2)

def filter_step(start, centre, half_width, blocks_diag, blocks_link):
    previous = start
    current = (apply_hamiltonian(start, blocks_diag, blocks_link) - centre * start) / half_width
    for degree_index in range(DEG - 1):
        following = 2.0 * (apply_hamiltonian(current, blocks_diag, blocks_link) - centre * current) / half_width - previous
        previous = current
        current = following
    return current

def orthonormal(filtered_block):
    flat = filtered_block.reshape(SLICES, K, ORDER)
    gram = jnp.einsum('skn,sjn->skj', flat, flat, precision=lax.Precision.HIGHEST) / ORDER
    factor = jnp.linalg.cholesky(gram)
    solved = lax.linalg.triangular_solve(factor, flat, left_side=True, lower=True)
    return solved

def reference(vectors, diag_blocks, couplings, bounds):
    blocks_diag = diag_blocks.astype(jnp.float32)
    blocks_link = couplings.astype(jnp.float32)
    bottom = bounds[:, 0].astype(jnp.float32) / 64.0
    summit = bounds[:, 1].astype(jnp.float32) / 64.0
    centre = ((bottom + summit) / 2.0).reshape(SLICES, 1, 1, 1)
    half_width = ((summit - bottom) / 2.0).reshape(SLICES, 1, 1, 1)
    current_block = vectors
    for repeat in range(STEPS):
        filtered_block = filter_step(current_block, centre, half_width, blocks_diag, blocks_link)
        final = orthonormal(filtered_block)
        current_block = final.reshape(SLICES, K, NL, B)
    low_edge = final[:, :EDGE]
    high_edge = final[:, K - EDGE:]
    zero_slice = jnp.zeros_like(low_edge[:1])
    below_high = jnp.concatenate([zero_slice, high_edge[:-1]], 0)
    above_low = jnp.concatenate([low_edge[1:], zero_slice], 0)
    correlation_low = jnp.einsum('swn,svn->swv', below_high, low_edge, precision=lax.Precision.HIGHEST) / ORDER
    correlation_high = jnp.einsum('swn,svn->swv', above_low, high_edge, precision=lax.Precision.HIGHEST) / ORDER
    low_new = low_edge - jnp.einsum('swv,swn->svn', correlation_low, below_high, precision=lax.Precision.HIGHEST)
    high_new = high_edge - jnp.einsum('swv,swn->svn', correlation_high, above_low, precision=lax.Precision.HIGHEST)
    result = jnp.concatenate([low_new, final[:, EDGE:K - EDGE], high_new], 1)
    return result.reshape(SLICES, K, NL, B)
```

```python
import functools

import jax
import jax.numpy as jnp
from jax import lax
from jax.experimental import pallas as pl
from jax.experimental.pallas import tpu as pltpu
from jax.sharding import PartitionSpec as P

EDGE = 16
DEG = 4
HIGHEST = lax.Precision.HIGHEST


def shifted(block, axis, distance):
    devices = range(lax.axis_size(axis))
    route = [(i - distance, i) for i in devices if i - distance in devices]
    return lax.ppermute(block, axis, route)


def swapped(block, axis, first):
    route = []
    for i in range(first, lax.axis_size(axis) - 1, 2):
        route += [(i, i + 1), (i + 1, i)]
    return lax.ppermute(block, axis, route)


def summed(block, axis):
    size = lax.axis_size(axis)
    if size & (size - 1) or size == 1:
        return lax.psum(block, axis)
    block = block + swapped(block, axis, 0)
    if size <= 8:
        others = [
            lax.ppermute(block, axis, [(i, i ^ step) for i in range(size)])
            for step in range(2, size, 2)
        ]
        for other in others:
            block = block + other
        return block
    step = 2
    while step < size:
        block = block + lax.ppermute(block, axis, [(i, i ^ step) for i in range(size)])
        step *= 2
    return block


def inner_products(first, second):
    return jnp.einsum("kn,jn->kj", first, second, precision=HIGHEST)


def inverse_factor(gram):
    size = gram.shape[0]
    row = lax.broadcasted_iota(jnp.int32, (size, size), 0)
    column = lax.broadcasted_iota(jnp.int32, (size, size), 1)
    work = jnp.concatenate([gram, jnp.where(row == column, 1.0, 0.0)], 1)
    below = lax.broadcasted_iota(jnp.int32, (size, 1), 0)
    pivots = jnp.zeros((size, 1), jnp.float32)
    for j in range(size):
        pivot_row = work[j : j + 1]
        pivot = pivot_row[:, j : j + 1]
        factor = jnp.where(below > j, work[:, j : j + 1] / pivot, 0.0)
        pivots = jnp.where(below == j, pivot, pivots)
        work = work - factor * pivot_row
    return lax.rsqrt(pivots) * work[:, size:]


def factor_kernel(gram_ref, inverse_ref):
    inverse_ref[...] = inverse_factor(gram_ref[...])


def final_kernel(edge, gram_ref, below_gram_ref, above_gram_ref, below_cross_ref, above_cross_ref, out_ref):
    dot = functools.partial(jnp.dot, precision=HIGHEST, preferred_element_type=jnp.float32)
    size = gram_ref.shape[0]
    own = inverse_factor(gram_ref[...])
    below = inverse_factor(below_gram_ref[...])[size - edge :]
    above = inverse_factor(above_gram_ref[...])
    low_t = dot(dot(own[:edge, :edge], below_cross_ref[...].T), below.T)
    high_t = dot(dot(own[size - edge :], above_cross_ref[...].T), above.T)
    out_ref[:, :size] = own
    out_ref[:, size:] = jnp.zeros((size, size + edge), jnp.float32)
    out_ref[:edge, size : 2 * size] = -dot(low_t, below)
    out_ref[size - edge :, 2 * size :] = -dot(high_t, above)


def per_device(vectors, diag_blocks, couplings, bounds):
    count_vec, layers, width = vectors.shape[1:]
    length_all = lax.axis_size("layer") * layers * width
    bottom = bounds[0, 0].astype(jnp.float32) / 64.0
    summit = bounds[0, 1].astype(jnp.float32) / 64.0
    centre = (bottom + summit) / 2.0
    half_width = (summit - bottom) / 2.0
    even = lax.axis_index("layer") % 2 == 0

    def product(block, matrix):
        return jnp.dot(block, matrix, preferred_element_type=jnp.float32)

    def product_t(block, matrix):
        return lax.dot_general(
            block, matrix, (((1,), (1,)), ((), ())), preferred_element_type=jnp.float32
        )

    def apply_operator(now):
        rounded = [block.astype(jnp.bfloat16) for block in now]
        tail = product(rounded[-1], couplings[layers - 1]).astype(jnp.bfloat16)
        outer = swapped(jnp.where(even, rounded[0], tail), "layer", 1)
        inner = swapped(jnp.where(even, tail, rounded[0]), "layer", 0)
        result = [product(rounded[l], diag_blocks[l]) for l in range(layers)]
        for l in range(layers - 1):
            result[l] = result[l] + product_t(rounded[l + 1], couplings[l])
            result[l + 1] = result[l + 1] + product(rounded[l], couplings[l])
        result[0] = result[0] + jnp.where(even, outer, inner).astype(jnp.float32)
        following = jnp.where(even, inner, outer)
        result[-1] = result[-1] + product_t(following, couplings[layers - 1])
        return result

    def filter_block(start):
        previous = start
        image = apply_operator(start)
        current = [(image[l] - centre * start[l]) / half_width for l in range(layers)]
        for degree_index in range(DEG - 1):
            image = apply_operator(current)
            following = [
                2.0 * (image[l] - centre * current[l]) / half_width - previous[l]
                for l in range(layers)
            ]
            previous = current
            current = following
        return current

    def gram_of(blocks):
        return sum(inner_products(block, block) for block in blocks)

    current = filter_block([vectors[0, :, l] for l in range(layers)])
    gram = summed(gram_of(current), "layer") / length_all
    inverse = pl.pallas_call(
        factor_kernel, out_shape=jax.ShapeDtypeStruct(gram.shape, jnp.float32)
    )(gram)
    current = [jnp.dot(inverse, block, precision=HIGHEST) for block in current]
    current = filter_block(current)

    flat = jnp.concatenate(current, 1)
    rounded = flat.astype(jnp.bfloat16)
    below = shifted(rounded, "cuts", 1)
    above = shifted(rounded[:EDGE], "cuts", -1)
    own_gram = inner_products(flat, flat)
    below_wide = below.astype(jnp.float32)
    above_wide = above.astype(jnp.float32)
    parts = [
        own_gram,
        product_t(below, below),
        inner_products(flat, above_wide),
        inner_products(below_wide, flat[:EDGE]),
        jnp.pad(product_t(above, above), ((0, count_vec - EDGE), (0, 0))),
    ]
    total = summed(jnp.concatenate(parts, 1), "layer") / length_all
    slice_at = lax.axis_index("cuts")
    gram = total[:, :count_vec]
    below_gram = jnp.where(slice_at > 0, total[:, count_vec : 2 * count_vec], jnp.eye(count_vec))
    rest = total[:, 2 * count_vec :]
    above_gram = jnp.where(
        slice_at < lax.axis_size("cuts") - 1, rest[:EDGE, 2 * EDGE :], jnp.eye(EDGE)
    )
    weights = pl.pallas_call(
        functools.partial(final_kernel, EDGE),
        out_shape=jax.ShapeDtypeStruct((count_vec, 2 * count_vec + EDGE), jnp.float32),
    )(gram, below_gram, above_gram, rest[:, EDGE : 2 * EDGE], rest[:, :EDGE].T)
    stacked = jnp.concatenate([flat, below_wide, above_wide], 0)
    result = jnp.dot(weights, stacked, precision=HIGHEST)
    return result.reshape(1, count_vec, layers, width)


def solution(mesh):
    in_specs = (
        P("cuts", None, "layer", None),
        P("layer", None, None),
        P("layer", None, None),
        P("cuts", None),
    )
    out_specs = P("cuts", None, "layer", None)
    return jax.shard_map(
        per_device, mesh=mesh, in_specs=in_specs, out_specs=out_specs, check_vma=False
    )
```

```python
import functools

import jax
import jax.numpy as jnp
from jax import lax
from jax.experimental import pallas as pl
from jax.experimental.pallas import tpu as pltpu
from jax.sharding import PartitionSpec as P

EDGE = 16
DEG = 4
ROWS = 8
HIGHEST = lax.Precision.HIGHEST
BF16 = jnp.bfloat16
F32 = jnp.float32
VMEM = pl.BlockSpec(memory_space=pltpu.VMEM)
SMEM = pl.BlockSpec(memory_space=pltpu.SMEM)


def exchanged(block, first):
    count, slices = lax.axis_size("layer"), lax.axis_size("cuts")
    route = []
    for cut in range(slices):
        for i in range(count):
            j = i + 1 if (i - first) % 2 == 0 else i - 1
            to = (cut, j) if 0 <= j < count else (cut ^ 1 if cut ^ 1 < slices else cut, i)
            route.append((cut * count + i, to[0] * count + to[1]))
    return lax.ppermute(block, ("cuts", "layer"), route)


def rotated(block, distance):
    size = lax.axis_size("cuts")
    return lax.ppermute(block, "cuts", [(i, (i + distance) % size) for i in range(size)])


def partial_sums(block):
    size = lax.axis_size("layer")
    if size & (size - 1) or size == 1:
        return [lax.psum(block, "layer")]
    block = block + lax.ppermute(block, "layer", [(i, i ^ 1) for i in range(size)])
    reach = 2
    while size // reach > 4:
        block = block + lax.ppermute(block, "layer", [(i, i ^ reach) for i in range(size)])
        reach *= 2
    return [block] + [
        lax.ppermute(block, "layer", [(i, i ^ step) for i in range(size)])
        for step in range(reach, size, reach)
    ]


def product(block, matrix):
    return jnp.dot(block, matrix, preferred_element_type=F32)


def product_t(block, matrix, precision=None):
    return lax.dot_general(
        block, matrix, (((1,), (1,)), ((), ())), precision=precision, preferred_element_type=F32
    )


def exact(first, second):
    return jnp.dot(first, second, precision=HIGHEST, preferred_element_type=F32)


def inverse_factor(gram):
    size = gram.shape[0]
    row = lax.broadcasted_iota(jnp.int32, (size, size), 0)
    column = lax.broadcasted_iota(jnp.int32, (size, size), 1)
    work = jnp.concatenate([jnp.where(row == column, 1.0, 0.0), gram], 1)
    finished = []
    for start in range(0, size, ROWS):
        left = size - start
        at = lax.broadcasted_iota(jnp.int32, (left, 2 * size), 0)
        lines = [
            jnp.broadcast_to(work[:, size + start + c : size + start + c + 1], (left, 2 * size))
            for c in range(ROWS)
        ]
        pivots = jnp.zeros((ROWS, 2 * size), F32)
        for c in range(ROWS):
            pivot = lines[c][c : c + 1]
            factor = jnp.where(at > c, lines[c] * (1.0 / pivot), 0.0)
            pivots = jnp.where(at[:ROWS] == c, pivot, pivots)
            work = work - factor * work[c : c + 1]
            for d in range(c + 1, ROWS):
                lines[d] = lines[d] - factor * lines[d][c : c + 1]
        finished.append(lax.rsqrt(pivots) * work[:ROWS])
        work = work[ROWS:]
    return jnp.concatenate(finished, 0)[:, :size]


def send(at, rounded_ref, coupling, inner_ref, outer_ref):
    last = rounded_ref.shape[0] - 1
    tail = product(rounded_ref[last], coupling).astype(BF16)
    first = rounded_ref[0]

    @pl.when(at % 2 == 0)
    def _():
        inner_ref[...] = tail
        outer_ref[...] = first

    @pl.when(at % 2 == 1)
    def _():
        inner_ref[...] = first
        outer_ref[...] = tail


def enter_kernel(at_ref, vectors_ref, couplings_ref, start_ref, rounded_ref, inner_ref, outer_ref):
    layers = start_ref.shape[0]
    for l in range(layers):
        block = vectors_ref[:, l, :]
        start_ref[l] = block
        rounded_ref[l] = block.astype(BF16)
    send(at_ref[0], rounded_ref, couplings_ref[layers - 1], inner_ref, outer_ref)


def interior_kernel(at_ref, rounded_ref, arrived_ref, diag_ref, couplings_ref, sum_ref):
    layers = rounded_ref.shape[0]
    for l in range(layers):
        term = product(rounded_ref[l], diag_ref[l])
        if l > 0:
            term = term + product(rounded_ref[l - 1], couplings_ref[l - 1])
        if l < layers - 1:
            term = term + product_t(rounded_ref[l + 1], couplings_ref[l])
        sum_ref[l] = term

    @pl.when(at_ref[0] % 2 == 0)
    def _():
        sum_ref[layers - 1] += product_t(arrived_ref[...], couplings_ref[layers - 1])

    @pl.when(at_ref[0] % 2 == 1)
    def _():
        sum_ref[0] += arrived_ref[...].astype(F32)


def advance(count, first_step, at, shift_ref, sum_ref, arrived_ref, couplings_ref, now_ref, before_ref, next_ref):
    layers = sum_ref.shape[0]

    @pl.when((at % 2 == 0) & (at > 0))
    def _():
        sum_ref[0] += arrived_ref[...].astype(F32)

    @pl.when((at % 2 == 1) & (at < count - 1))
    def _():
        sum_ref[layers - 1] += product_t(arrived_ref[...], couplings_ref[layers - 1])

    centre, scale = shift_ref[0], shift_ref[1]
    for l in range(layers):
        block = (sum_ref[l] - centre * now_ref[l]) * scale
        if not first_step:
            block = 2.0 * block - before_ref[l]
        next_ref[l] = block


def step_kernel(
    count, first_step, at_ref, shift_ref, sum_in_ref, arrived_ref, couplings_ref, now_ref, before_ref,
    next_ref, rounded_ref, inner_ref, outer_ref, sum_ref,
):
    at = at_ref[0]
    sum_ref[...] = sum_in_ref[...]
    advance(
        count, first_step, at, shift_ref, sum_ref, arrived_ref, couplings_ref, now_ref, before_ref, next_ref
    )
    rounded_ref[...] = next_ref[...].astype(BF16)
    send(at, rounded_ref, couplings_ref[sum_ref.shape[0] - 1], inner_ref, outer_ref)


def last_kernel(
    count, at_ref, shift_ref, sum_in_ref, arrived_ref, couplings_ref, now_ref, before_ref,
    next_ref, rounded_ref, gram_ref, sum_ref,
):
    sum_ref[...] = sum_in_ref[...]
    advance(
        count, False, at_ref[0], shift_ref, sum_ref, arrived_ref, couplings_ref, now_ref, before_ref, next_ref
    )
    rounded_ref[...] = next_ref[...].astype(BF16)
    gram_ref[...] = sum(
        product_t(next_ref[l], next_ref[l], HIGHEST) for l in range(next_ref.shape[0])
    )


def normal_kernel(parts, length, at_ref, *refs):
    grams, (filtered_ref, couplings_ref, start_ref, rounded_ref, inner_ref, outer_ref) = refs[:parts], refs[parts:]
    gram = sum(ref[...] for ref in grams) * (1.0 / length)
    inverse = inverse_factor(gram)
    layers = start_ref.shape[0]
    for l in range(layers):
        block = exact(inverse, filtered_ref[l])
        start_ref[l] = block
        rounded_ref[l] = block.astype(BF16)
    send(at_ref[0], rounded_ref, couplings_ref[layers - 1], inner_ref, outer_ref)


def cross_kernel(gram_ref, rounded_ref, below_ref, above_ref, out_ref):
    size, edge = gram_ref.shape[0], above_ref.shape[1]
    layers = range(rounded_ref.shape[0])
    out_ref[:, :size] = gram_ref[...]
    out_ref[:, size : 2 * size] = sum(product_t(below_ref[l], below_ref[l]) for l in layers)
    out_ref[:, 2 * size : 2 * size + edge] = sum(
        product_t(below_ref[l], rounded_ref[l, :edge]) for l in layers
    )
    out_ref[:, 2 * size + edge : 2 * size + 2 * edge] = sum(
        product_t(rounded_ref[l], above_ref[l]) for l in layers
    )
    out_ref[:edge, 2 * size + 2 * edge :] = sum(
        product_t(above_ref[l], above_ref[l]) for l in layers
    )
    out_ref[edge:, 2 * size + 2 * edge :] = jnp.zeros((size - edge, edge), F32)


def final_kernel(parts, length, slices, cut_ref, *refs):
    grams, (filtered_ref, below_ref, above_ref, out_ref) = refs[:parts], refs[parts:]
    layers, size, _ = filtered_ref.shape
    edge = above_ref.shape[1]
    total = sum(ref[...] for ref in grams) * (1.0 / length)

    def identity(extent):
        row = lax.broadcasted_iota(jnp.int32, (extent, extent), 0)
        column = lax.broadcasted_iota(jnp.int32, (extent, extent), 1)
        return jnp.where(row == column, 1.0, 0.0)

    has_below = (cut_ref[0] > 0).astype(F32)
    has_above = (cut_ref[0] < slices - 1).astype(F32)
    below_gram = total[:, size : 2 * size] * has_below + identity(size) * (1.0 - has_below)
    above_gram = total[:edge, 2 * size + 2 * edge :] * has_above + identity(edge) * (1.0 - has_above)
    below_cross = total[:, 2 * size : 2 * size + edge] * has_below
    above_cross = total[:, 2 * size + edge : 2 * size + 2 * edge] * has_above
    own = inverse_factor(total[:, :size])
    below = inverse_factor(below_gram)[size - edge :]
    above = inverse_factor(above_gram)
    low_t = exact(own[:edge, :edge], product_t(below_cross.T, below, HIGHEST))
    high_t = exact(own[size - edge :], product_t(above_cross, above, HIGHEST))
    low_weights = exact(low_t, below)
    high_weights = exact(high_t, above)
    for l in range(layers):
        block = exact(own, filtered_ref[l])
        out_ref[:edge, l, :] = block[:edge] - exact(low_weights, below_ref[l].astype(F32))
        out_ref[edge : size - edge, l, :] = block[edge : size - edge]
        out_ref[size - edge :, l, :] = block[size - edge :] - exact(
            high_weights, above_ref[l].astype(F32)
        )


def per_device(vectors, diag_blocks, couplings, bounds):
    vectors = vectors[0]
    count_vec, layers, width = vectors.shape
    count = lax.axis_size("layer")
    length_all = count * layers * width
    low = bounds[0, 0].astype(F32) / 64.0
    high = bounds[0, 1].astype(F32) / 64.0
    shift = jnp.stack([(low + high) / 2.0, 2.0 / (high - low)])
    at = lax.axis_index("layer").astype(jnp.int32).reshape(1)
    cut = lax.axis_index("cuts").astype(jnp.int32).reshape(1)

    field = (layers, count_vec, width)
    field32 = jax.ShapeDtypeStruct(field, F32)
    field16 = jax.ShapeDtypeStruct(field, BF16)
    message = jax.ShapeDtypeStruct((count_vec, width), BF16)
    gram_type = jax.ShapeDtypeStruct((count_vec, count_vec), F32)
    scratch = [pltpu.VMEM(field, F32)]

    def call(kernel, outs, scalars, *operands, scratch_shapes=(), flops=0):
        moved = sum(x.size * x.dtype.itemsize for x in operands)
        return pl.pallas_call(
            kernel,
            out_shape=outs,
            in_specs=[SMEM] * len(scalars) + [VMEM] * len(operands),
            out_specs=jax.tree.map(lambda _: VMEM, outs),
            scratch_shapes=list(scratch_shapes),
            compiler_params=pltpu.CompilerParams(vmem_limit_bytes=32 * 2**20),
            cost_estimate=pl.CostEstimate(flops=flops, bytes_accessed=moved, transcendentals=0),
        )(*scalars, *operands)

    one = 2 * count_vec * width * width

    def filter_block(start, rounded, inner, outer):
        before, now = start, start
        for step in range(DEG):
            outer_in = exchanged(outer, 1)
            inner_in = exchanged(inner, 0)
            partial = call(
                interior_kernel, field32, [at], rounded, inner_in, diag_blocks, couplings,
                flops=(3 * layers - 1) * one,
            )
            operands = (partial, outer_in, couplings, now, before)
            if step < DEG - 1:
                following, rounded, inner, outer = call(
                    functools.partial(step_kernel, count, step == 0),
                    (field32, field16, message, message), [at, shift], *operands,
                    scratch_shapes=scratch, flops=2 * one,
                )
                before, now = now, following
            else:
                return call(
                    functools.partial(last_kernel, count),
                    (field32, field16, gram_type), [at, shift], *operands,
                    scratch_shapes=scratch, flops=2 * one,
                )

    outs = (field32, field16, message, message)
    start = call(enter_kernel, outs, [at], vectors, couplings, flops=one)
    filtered, rounded, gram = filter_block(*start)
    grams = partial_sums(gram)
    start = call(
        functools.partial(normal_kernel, len(grams), length_all), outs, [at], *grams, filtered, couplings,
        flops=2 * one,
    )
    filtered, rounded, gram = filter_block(*start)
    below = rotated(rounded, 1)
    above = rotated(rounded[:, :EDGE], -1)
    cross = call(
        cross_kernel, jax.ShapeDtypeStruct((count_vec, 2 * count_vec + 3 * EDGE), F32), [],
        gram, rounded, below, above,
    )
    grams = partial_sums(cross)
    result = call(
        functools.partial(final_kernel, len(grams), length_all, lax.axis_size("cuts")),
        jax.ShapeDtypeStruct((count_vec, layers, width), F32), [cut], *grams, filtered, below, above,
    )
    return result[None]


def solution(mesh):
    in_specs = (
        P("cuts", None, "layer", None),
        P("layer", None, None),
        P("layer", None, None),
        P("cuts", None),
    )
    out_specs = P("cuts", None, "layer", None)
    return jax.shard_map(
        per_device, mesh=mesh, in_specs=in_specs, out_specs=out_specs, check_vma=False
    )
```

```python
import functools

import jax
import jax.numpy as jnp
from jax import lax
from jax.experimental import pallas as pl
from jax.experimental.pallas import tpu as pltpu
from jax.sharding import PartitionSpec as P

EDGE = 16
DEG = 4
ROWS = 8
HIGHEST = lax.Precision.HIGHEST
BF16 = jnp.bfloat16
F32 = jnp.float32
VMEM = pl.BlockSpec(memory_space=pltpu.VMEM)
SMEM = pl.BlockSpec(memory_space=pltpu.SMEM)
HBM = pl.BlockSpec(memory_space=pltpu.HBM)


def exchanged(block, first):
    count, slices = lax.axis_size("layer"), lax.axis_size("cuts")
    route = []
    for cut in range(slices):
        for i in range(count):
            j = i + 1 if (i - first) % 2 == 0 else i - 1
            to = (cut, j) if 0 <= j < count else (cut ^ 1 if cut ^ 1 < slices else cut, i)
            route.append((cut * count + i, to[0] * count + to[1]))
    return lax.ppermute(block, ("cuts", "layer"), route)


def rotated(block, distance):
    size = lax.axis_size("cuts")
    return lax.ppermute(block, "cuts", [(i, (i + distance) % size) for i in range(size)])


def partial_sums(block):
    size = lax.axis_size("layer")
    if size & (size - 1) or size == 1:
        return [lax.psum(block, "layer")]
    block = block + lax.ppermute(block, "layer", [(i, i ^ 1) for i in range(size)])
    reach = 2
    while size // reach > 4:
        block = block + lax.ppermute(block, "layer", [(i, i ^ reach) for i in range(size)])
        reach *= 2
    return [block] + [
        lax.ppermute(block, "layer", [(i, i ^ step) for i in range(size)])
        for step in range(reach, size, reach)
    ]


def product(block, matrix):
    return jnp.dot(block, matrix, preferred_element_type=F32)


def product_t(block, matrix, precision=None):
    return lax.dot_general(
        block, matrix, (((1,), (1,)), ((), ())), precision=precision, preferred_element_type=F32
    )


def exact(first, second):
    return jnp.dot(first, second, precision=HIGHEST, preferred_element_type=F32)


def inverse_factor(gram):
    size = gram.shape[0]
    row = lax.broadcasted_iota(jnp.int32, (size, size), 0)
    column = lax.broadcasted_iota(jnp.int32, (size, size), 1)
    work = jnp.concatenate([jnp.where(row == column, 1.0, 0.0), gram], 1)
    finished = []
    for start in range(0, size, ROWS):
        left = size - start
        at = lax.broadcasted_iota(jnp.int32, (left, 2 * size), 0)
        lines = [
            jnp.broadcast_to(work[:, size + start + c : size + start + c + 1], (left, 2 * size))
            for c in range(ROWS)
        ]
        pivots = jnp.zeros((ROWS, 2 * size), F32)
        for c in range(ROWS):
            pivot = lines[c][c : c + 1]
            factor = jnp.where(at > c, lines[c] * (1.0 / pivot), 0.0)
            pivots = jnp.where(at[:ROWS] == c, pivot, pivots)
            work = work - factor * work[c : c + 1]
            for d in range(c + 1, ROWS):
                lines[d] = lines[d] - factor * lines[d][c : c + 1]
        finished.append(lax.rsqrt(pivots) * work[:ROWS])
        work = work[ROWS:]
    return jnp.concatenate(finished, 0)[:, :size]


def by_parity(at, body):
    @pl.when(at % 2 == 0)
    def _():
        body(False)

    @pl.when(at % 2 == 1)
    def _():
        body(True)


def scaled(bounds_ref, factor, width):
    low, high = bounds_ref[0].astype(F32), bounds_ref[1].astype(F32)
    half = jnp.full((1, width), (high - low) * (1.0 / 128.0), F32)
    return factor / half, (low + high) * (1.0 / 128.0)


def enter_kernel(
    at_ref, vectors_ref, couplings_ref,
    outer_ref, rest_ref, outer16_ref, rest16_ref, inner_send_ref, outer_send_ref, last_ref, last_t_ref,
    block_ref, sems,
):
    layers = vectors_ref.shape[1]
    vectors_copy = pltpu.make_async_copy(vectors_ref, block_ref, sems.at[0])
    last_copy = pltpu.make_async_copy(couplings_ref.at[layers - 1], last_ref, sems.at[1])
    vectors_copy.start()
    last_copy.start()
    vectors_copy.wait()

    def body(odd):
        outer = layers - 1 if odd else 0
        rest = [l for l in range(layers) if l != outer]
        outer_ref[...] = block_ref[:, outer, :]
        outer16_ref[...] = outer_ref[...].astype(BF16)
        for i, l in enumerate(rest):
            rest_ref[i] = block_ref[:, l, :]
            rest16_ref[i] = rest_ref[i].astype(BF16)

    by_parity(at_ref[0], body)
    last_copy.wait()

    def messages(odd):
        if odd:
            outer_send_ref[...] = product(outer16_ref[...], last_ref[...]).astype(BF16)
            inner_send_ref[...] = rest16_ref[0]
        else:
            outer_send_ref[...] = outer16_ref[...]
            inner_send_ref[...] = product(rest16_ref[layers - 2], last_ref[...]).astype(BF16)

    by_parity(at_ref[0], messages)
    last_t_ref[...] = jnp.transpose(last_ref[...])


def interior_kernel(
    layers, load, first_step, final, at_ref, bounds_ref, outer16_ref, rest16_ref, arrived_ref, diag_ref,
    last_ref, last_t_ref, *refs,
):
    if load:
        (couplings_ref, outer_ref, rest_ref, outer_before_ref, rest_before_ref, *outs, mid_ref, mid_t_ref, sem) = refs
        copy = pltpu.make_async_copy(couplings_ref.at[pl.ds(0, layers - 1)], mid_ref, sem)
        copy.start()
        copy.wait()
        for i in range(layers - 1):
            mid_t_ref[i] = jnp.transpose(mid_ref[i])
    else:
        (mid_ref, mid_t_ref, outer_ref, rest_ref, outer_before_ref, rest_before_ref, *outs) = refs
    base_ref, next_ref, next16_ref, last_out_ref = outs
    scale, centre = scaled(bounds_ref, 1.0 if first_step else 2.0, outer16_ref.shape[1])

    def body(odd):
        outer = layers - 1 if odd else 0
        rest = [l for l in range(layers) if l != outer]

        def rounded(l):
            return outer16_ref[...] if l == outer else rest16_ref[rest.index(l)]

        for l in rest + [outer]:
            term = product(rounded(l), diag_ref[l])
            if l > 0:
                term = term + product(rounded(l - 1), mid_ref[l - 1])
            if l < layers - 1:
                term = term + product(rounded(l + 1), mid_t_ref[l])
            if odd and l == 0:
                term = term + arrived_ref[...].astype(F32)
            if not odd and l == layers - 1:
                term = term + product(arrived_ref[...], last_t_ref[...])
            if l == outer:
                term = (term - centre * outer_ref[...]) * scale
                base_ref[...] = term if first_step else term - outer_before_ref[...]
            else:
                i = rest.index(l)
                term = (term - centre * rest_ref[i]) * scale
                term = term if first_step else term - rest_before_ref[i]
                next_ref[i] = term
                next16_ref[i] = term.astype(BF16)
        if final:
            last_out_ref[...] = sum(
                product_t(next_ref[i], next_ref[i], HIGHEST) for i in range(layers - 1)
            )
        elif odd:
            last_out_ref[...] = next16_ref[0]
        else:
            last_out_ref[...] = product(next16_ref[layers - 2], last_ref[...]).astype(BF16)

    by_parity(at_ref[0], body)


def finish(count, first_step, at, bounds_ref, base_ref, arrived_ref, last_t_ref, next_ref):
    scale, _ = scaled(bounds_ref, 1.0 if first_step else 2.0, next_ref.shape[1])

    def body(odd):
        @pl.when(at != (count - 1 if odd else 0))
        def _():
            arrived = arrived_ref[...]
            term = product(arrived, last_t_ref[...]) if odd else arrived.astype(F32)
            next_ref[...] = base_ref[...] + term * scale

        @pl.when(at == (count - 1 if odd else 0))
        def _():
            next_ref[...] = base_ref[...]

    by_parity(at, body)


def step_kernel(
    count, first_step, at_ref, bounds_ref, base_ref, arrived_ref, last_ref, last_t_ref,
    next_ref, next16_ref, send_ref,
):
    at = at_ref[0]
    finish(count, first_step, at, bounds_ref, base_ref, arrived_ref, last_t_ref, next_ref)
    next16_ref[...] = next_ref[...].astype(BF16)
    send_outer(at, next16_ref, last_ref, send_ref)


def send_outer(at, rounded_ref, last_ref, send_ref):
    def body(odd):
        if odd:
            send_ref[...] = product(rounded_ref[...], last_ref[...]).astype(BF16)
        else:
            send_ref[...] = rounded_ref[...]

    by_parity(at, body)


def last_kernel(
    count, at_ref, bounds_ref, base_ref, arrived_ref, last_t_ref, rest16_ref, rest_gram_ref,
    next_ref, next16_ref, low_ref, gram_ref,
):
    finish(count, False, at_ref[0], bounds_ref, base_ref, arrived_ref, last_t_ref, next_ref)
    edge = low_ref.shape[1]
    next16_ref[...] = next_ref[...].astype(BF16)
    low_ref[0] = next16_ref[:edge]
    for i in range(low_ref.shape[0] - 1):
        low_ref[i + 1] = rest16_ref[i, :edge]
    gram_ref[...] = rest_gram_ref[...] + product_t(next_ref[...], next_ref[...], HIGHEST)


def normal_kernel(parts, length, at_ref, *refs):
    grams, (filtered_ref, last_ref, inverse_ref, outer_ref, outer16_ref, send_ref) = refs[:parts], refs[parts:]
    inverse_ref[...] = inverse_factor(sum(ref[...] for ref in grams) * (1.0 / length))
    outer_ref[...] = exact(inverse_ref[...], filtered_ref[...])
    outer16_ref[...] = outer_ref[...].astype(BF16)
    send_outer(at_ref[0], outer16_ref, last_ref, send_ref)


def normal_rest_kernel(at_ref, inverse_ref, filtered_ref, last_ref, rest_ref, rest16_ref, send_ref):
    layers = rest_ref.shape[0]
    for i in range(layers):
        rest_ref[i] = exact(inverse_ref[...], filtered_ref[i])
        rest16_ref[i] = rest_ref[i].astype(BF16)

    def body(odd):
        if odd:
            send_ref[...] = rest16_ref[0]
        else:
            send_ref[...] = product(rest16_ref[layers - 1], last_ref[...]).astype(BF16)

    by_parity(at_ref[0], body)


def cross_kernel(gram_ref, outer16_ref, rest16_ref, above_ref, out_ref):
    size, edge = gram_ref.shape[0], above_ref.shape[1]
    rest = range(rest16_ref.shape[0])
    out_ref[:, :size] = gram_ref[...]
    out_ref[:, size : size + edge] = product_t(outer16_ref[...], above_ref[0]) + sum(
        product_t(rest16_ref[i], above_ref[i + 1]) for i in rest
    )
    out_ref[:edge, size + edge :] = sum(
        product_t(above_ref[l], above_ref[l]) for l in range(above_ref.shape[0])
    )
    out_ref[edge:, size + edge :] = jnp.zeros((size - edge, edge), F32)


def factor_kernel(parts, length, slices, cut_ref, *refs):
    grams, (outer_ref, rest_ref, inverse_ref, weights_ref, up_ref) = refs[:parts], refs[parts:]
    size, edge = outer_ref.shape[0], up_ref.shape[1]
    total = sum(ref[...] for ref in grams) * (1.0 / length)
    has_above = (cut_ref[0] < slices - 1).astype(F32)
    row = lax.broadcasted_iota(jnp.int32, (edge, edge), 0)
    column = lax.broadcasted_iota(jnp.int32, (edge, edge), 1)
    identity = jnp.where(row == column, 1.0, 0.0)
    above_gram = total[:edge, size + edge :] * has_above + identity * (1.0 - has_above)
    own = inverse_factor(total[:, :size])
    above = inverse_factor(above_gram)
    inverse_ref[...] = own
    high = own[size - edge :]
    correlation = product_t(exact(high, total[:, size : size + edge]), above, HIGHEST) * has_above
    weights_ref[...] = exact(correlation, above)
    up = exact(correlation.T, high)
    up_ref[0] = exact(up, outer_ref[...]).astype(BF16)
    for i in range(rest_ref.shape[0]):
        up_ref[i + 1] = exact(up, rest_ref[i]).astype(BF16)


def final_kernel(slices, at_ref, cut_ref, inverse_ref, weights_ref, outer_ref, rest_ref, above_ref, below_ref, out_ref):
    size, edge = outer_ref.shape[0], above_ref.shape[1]
    layers = above_ref.shape[0]
    has_below = (cut_ref[0] > 0).astype(F32)
    weights = weights_ref[...]

    def body(odd):
        outer = layers - 1 if odd else 0
        order = [outer] + [l for l in range(layers) if l != outer]
        for i, l in enumerate(order):
            block = exact(inverse_ref[...], outer_ref[...] if i == 0 else rest_ref[i - 1])
            out_ref[:edge, l, :] = block[:edge] - below_ref[i].astype(F32) * has_below
            out_ref[edge : size - edge, l, :] = block[edge : size - edge]
            out_ref[size - edge :, l, :] = block[size - edge :] - exact(
                weights, above_ref[i].astype(F32)
            )

    by_parity(at_ref[0], body)


def per_device(vectors, diag_blocks, couplings, bounds):
    vectors = vectors[0]
    count_vec, layers, width = vectors.shape
    count, slices = lax.axis_size("layer"), lax.axis_size("cuts")
    length_all = count * layers * width
    at = lax.axis_index("layer").astype(jnp.int32).reshape(1)
    cut = lax.axis_index("cuts").astype(jnp.int32).reshape(1)
    bounds = bounds[0]

    def array(dtype, *shape):
        return jax.ShapeDtypeStruct(shape, dtype)

    outer32, outer16 = array(F32, count_vec, width), array(BF16, count_vec, width)
    rest32, rest16 = array(F32, layers - 1, count_vec, width), array(BF16, layers - 1, count_vec, width)
    square = array(F32, count_vec, count_vec)
    matrix = array(BF16, width, width)
    matrices = array(BF16, layers - 1, width, width)
    edges = array(BF16, layers, EDGE, width)
    one = 2 * count_vec * width * width

    def call(kernel, outs, scalars, *operands, far=(), scratch_shapes=(), flops=one):
        moved = sum(x.size * x.dtype.itemsize for x in operands)
        return pl.pallas_call(
            kernel,
            out_shape=outs,
            in_specs=[SMEM] * len(scalars) + [HBM if i in far else VMEM for i in range(len(operands))],
            out_specs=jax.tree.map(lambda _: VMEM, outs),
            scratch_shapes=list(scratch_shapes),
            compiler_params=pltpu.CompilerParams(vmem_limit_bytes=32 * 2**20),
            cost_estimate=pl.CostEstimate(flops=flops, bytes_accessed=moved, transcendentals=0),
        )(*scalars, *operands)

    outer, rest, outer_r, rest_r, inner_send, outer_send, last, last_t = call(
        enter_kernel,
        (outer32, rest32, outer16, rest16, outer16, outer16, matrix, matrix),
        [at], vectors, couplings, far=(0, 1),
        scratch_shapes=[pltpu.VMEM(vectors.shape, F32), pltpu.SemaphoreType.DMA((2,))],
    )
    mid = mid_t = None

    def filter_block(outer, rest, outer_r, rest_r, inner_send, outer_send, mid, mid_t):
        outer_before, rest_before = outer, rest
        for step in range(DEG):
            final = step == DEG - 1
            outer_in = exchanged(outer_send, 1)
            inner_in = exchanged(inner_send, 0)
            load = mid is None
            middle = (couplings,) if load else (mid, mid_t)
            outs = (outer32, rest32, rest16, square if final else outer16)
            result = call(
                functools.partial(interior_kernel, layers, load, step == 0, final),
                outs + ((matrices, matrices) if load else ()),
                [at, bounds], outer_r, rest_r, inner_in, diag_blocks, last, last_t,
                *middle, outer, rest, outer_before, rest_before,
                far=(6,) if load else (),
                scratch_shapes=[pltpu.SemaphoreType.DMA] if load else [],
                flops=(3 * layers - 1) * one,
            )
            base, rest_next, rest_r, extra = result[:4]
            if load:
                mid, mid_t = result[4:]
            if final:
                outer_next, outer_r, low, gram = call(
                    functools.partial(last_kernel, count),
                    (outer32, outer16, edges, square),
                    [at, bounds], base, outer_in, last_t, rest_r, extra,
                )
                return outer_next, rest_next, outer_r, rest_r, low, gram, mid, mid_t
            inner_send = extra
            outer_next, outer_r, outer_send = call(
                functools.partial(step_kernel, count, step == 0),
                (outer32, outer16, outer16),
                [at, bounds], base, outer_in, last, last_t,
            )
            outer_before, rest_before, outer, rest = outer, rest, outer_next, rest_next

    outer, rest, _, _, _, gram, mid, mid_t = filter_block(
        outer, rest, outer_r, rest_r, inner_send, outer_send, mid, mid_t
    )
    grams = partial_sums(gram)
    inverse, outer, outer_r, outer_send = call(
        functools.partial(normal_kernel, len(grams), length_all),
        (square, outer32, outer16, outer16), [at], *grams, outer, last,
    )
    rest, rest_r, inner_send = call(
        normal_rest_kernel, (rest32, rest16, outer16), [at], inverse, rest, last
    )
    outer, rest, outer_r, rest_r, low, gram, _, _ = filter_block(
        outer, rest, outer_r, rest_r, inner_send, outer_send, mid, mid_t
    )
    above = rotated(low, -1)
    cross = call(
        cross_kernel, array(F32, count_vec, count_vec + 2 * EDGE), [], gram, outer_r, rest_r, above
    )
    grams = partial_sums(cross)
    inverse, weights, up = call(
        functools.partial(factor_kernel, len(grams), length_all, slices),
        (square, array(F32, EDGE, EDGE), edges), [cut], *grams, outer, rest,
    )
    below = rotated(up, 1)
    result = call(
        functools.partial(final_kernel, slices),
        array(F32, count_vec, layers, width), [at, cut], inverse, weights, outer, rest, above, below,
    )
    return result[None]


def solution(mesh):
    in_specs = (
        P("cuts", None, "layer", None),
        P("layer", None, None),
        P("layer", None, None),
        P("cuts", None),
    )
    out_specs = P("cuts", None, "layer", None)
    return jax.shard_map(
        per_device, mesh=mesh, in_specs=in_specs, out_specs=out_specs, check_vma=False
    )
```

```python
import functools

import jax
import jax.numpy as jnp
from jax import lax
from jax.experimental import pallas as pl
from jax.experimental.pallas import tpu as pltpu
from jax.sharding import PartitionSpec as P

EDGE = 16
DEG = 4
ROWS = 8
HIGHEST = lax.Precision.HIGHEST
BF16 = jnp.bfloat16
F32 = jnp.float32
VMEM = pl.BlockSpec(memory_space=pltpu.VMEM)
HBM = pl.BlockSpec(memory_space=pltpu.HBM)


def exchanged(block, first):
    count, slices = lax.axis_size("layer"), lax.axis_size("cuts")
    route = []
    for cut in range(slices):
        for i in range(count):
            j = i + 1 if (i - first) % 2 == 0 else i - 1
            to = (cut, j) if 0 <= j < count else (cut ^ 1 if cut ^ 1 < slices else cut, i)
            route.append((cut * count + i, to[0] * count + to[1]))
    return lax.ppermute(block, ("cuts", "layer"), route)


def far_away(block):
    return pltpu.with_memory_space_constraint(block, pltpu.HBM)


def rotated(block, distance):
    size = lax.axis_size("cuts")
    return lax.ppermute(block, "cuts", [(i, (i + distance) % size) for i in range(size)])


def partial_sums(block):
    size = lax.axis_size("layer")
    if size & (size - 1) or size == 1:
        return [lax.psum(block, "layer")]
    block = block + lax.ppermute(block, "layer", [(i, i ^ 1) for i in range(size)])
    reach = 2
    while size // reach > 4:
        block = block + lax.ppermute(block, "layer", [(i, i ^ reach) for i in range(size)])
        reach *= 2
    return [block] + [
        lax.ppermute(block, "layer", [(i, i ^ step) for i in range(size)])
        for step in range(reach, size, reach)
    ]


def product(block, matrix):
    return jnp.dot(block, matrix, preferred_element_type=F32)


def product_t(block, matrix, precision=None):
    return lax.dot_general(
        block, matrix, (((1,), (1,)), ((), ())), precision=precision, preferred_element_type=F32
    )


def exact(first, second):
    return jnp.dot(first, second, precision=HIGHEST, preferred_element_type=F32)


def inverse_factor(gram):
    size = gram.shape[0]
    row = lax.broadcasted_iota(jnp.int32, (size, size), 0)
    column = lax.broadcasted_iota(jnp.int32, (size, size), 1)
    work = jnp.concatenate([jnp.where(row == column, 1.0, 0.0), gram], 1)
    finished = []
    for start in range(0, size, ROWS):
        left = size - start
        at = lax.broadcasted_iota(jnp.int32, (left, 2 * size), 0)
        lines = [
            jnp.broadcast_to(work[:, size + start + c : size + start + c + 1], (left, 2 * size))
            for c in range(ROWS)
        ]
        pivots = jnp.zeros((ROWS, 2 * size), F32)
        for c in range(ROWS):
            pivot = lines[c][c : c + 1]
            factor = jnp.where(at > c, lines[c] * (1.0 / pivot), 0.0)
            pivots = jnp.where(at[:ROWS] == c, pivot, pivots)
            work = work - factor * work[c : c + 1]
            for d in range(c + 1, ROWS):
                lines[d] = lines[d] - factor * lines[d][c : c + 1]
        finished.append(lax.rsqrt(pivots) * work[:ROWS])
        work = work[ROWS:]
    return jnp.concatenate(finished, 0)[:, :size]


def position(axis):
    return lax.axis_index(axis).astype(jnp.int32)


def send_outer(odd, rounded_ref, last_ref, send_ref):
    @pl.when(odd == 0)
    def _():
        send_ref[...] = rounded_ref[...]

    @pl.when(odd == 1)
    def _():
        send_ref[...] = product(rounded_ref[...], last_ref[...]).astype(BF16)


def send_inner(odd, rounded_ref, last_ref, send_ref):
    end = rounded_ref.shape[0] - 1

    @pl.when(odd == 1)
    def _():
        send_ref[...] = rounded_ref[end]

    @pl.when(odd == 0)
    def _():
        send_ref[...] = product(rounded_ref[end], last_ref[...]).astype(BF16)


def enter_kernel(
    far_bounds_ref, vectors_ref, couplings_ref,
    outer_ref, rest_ref, outer16_ref, rest16_ref, inner_send_ref, outer_send_ref, last_ref, mids_ref, rows_ref,
    bounds_ref, block_ref, sems,
):
    layers = vectors_ref.shape[1]
    copies = [
        pltpu.make_async_copy(vectors_ref, block_ref, sems.at[0]),
        pltpu.make_async_copy(couplings_ref.at[layers - 1], last_ref, sems.at[1]),
        pltpu.make_async_copy(couplings_ref.at[pl.ds(0, layers - 1)], mids_ref, sems.at[2]),
        pltpu.make_async_copy(far_bounds_ref, bounds_ref, sems.at[3]),
    ]
    for copy in copies:
        copy.start()
    odd = position("layer") % 2
    copies[0].wait()
    for parity in (0, 1):

        @pl.when(odd == parity)
        def _():
            order = range(layers)[:: -1 if parity else 1]
            outer_ref[...] = block_ref[:, order[0], :]
            for i, l in enumerate(order[1:]):
                rest_ref[i] = block_ref[:, l, :]

    outer16_ref[...] = outer_ref[...].astype(BF16)
    rest16_ref[...] = rest_ref[...].astype(BF16)
    copies[1].wait()
    send_outer(odd, outer16_ref, last_ref, outer_send_ref)
    send_inner(odd, rest16_ref, last_ref, inner_send_ref)
    copies[3].wait()
    width = rows_ref.shape[1]
    low, high = bounds_ref[0, 0].astype(F32), bounds_ref[0, 1].astype(F32)
    half = jnp.full((1, width), (high - low) * (1.0 / 128.0), F32)
    rows_ref[0:1] = jnp.full((1, width), (low + high) * (1.0 / 128.0), F32)
    rows_ref[1:2] = 1.0 / half
    rows_ref[2:3] = 2.0 / half
    copies[2].wait()


def interior_kernel(
    layers, load, first_step, final, rows_ref, outer16_ref, rest16_ref, arrived_ref, diag_ref, last_ref, mids_ref, *refs,
):
    *refs, sum_ref = refs
    if load:
        (outer_ref, rest_ref, outer_before_ref, rest_before_ref, *outs, last_t_ref, mids_t_ref) = refs
        last_t_ref[...] = jnp.transpose(last_ref[...])
        for i in range(layers - 1):
            mids_t_ref[i] = jnp.transpose(mids_ref[i])
    else:
        (last_t_ref, mids_t_ref, outer_ref, rest_ref, outer_before_ref, rest_before_ref, *outs) = refs
    base_ref, next_ref, next16_ref, last_out_ref = outs
    centre, scale = rows_ref[0:1], rows_ref[1:2] if first_step else rows_ref[2:3]
    odd = position("layer") % 2

    def rounded(place):
        return rest16_ref[place - 1] if place else outer16_ref[...]

    def add(block, straight, link):
        @pl.when(odd == straight)
        def _():
            sum_ref[...] += product(block, mids_ref[link])

        @pl.when(odd != straight)
        def _():
            sum_ref[...] += product(block, mids_t_ref[link])

    for place in range(layers)[::-1]:
        sum_ref[...] = product(rounded(place), diag_ref[place + odd * (layers - 1 - 2 * place)])
        if place < layers - 1:
            add(rounded(place + 1), 1, place + odd * (layers - 2 - 2 * place))
        if place > 0:
            add(rounded(place - 1), 0, place - 1 + odd * (layers - 2 * place))
        if place == layers - 1:

            @pl.when(odd == 0)
            def _():
                sum_ref[...] += product(arrived_ref[...], last_t_ref[...])

            @pl.when(odd == 1)
            def _():
                sum_ref[...] += arrived_ref[...].astype(F32)

        if place:
            term = (sum_ref[...] - centre * rest_ref[place - 1]) * scale
            term = term if first_step else term - rest_before_ref[place - 1]
            next_ref[place - 1] = term
            next16_ref[place - 1] = term.astype(BF16)
        else:
            term = (sum_ref[...] - centre * outer_ref[...]) * scale
            base_ref[...] = term if first_step else term - outer_before_ref[...]
    if final:
        last_out_ref[...] = sum(
            product_t(next_ref[i], next_ref[i], HIGHEST) for i in range(layers - 1)
        )
    else:
        send_inner(odd, next16_ref, last_ref, last_out_ref)


def finish(count, first_step, rows_ref, base_ref, arrived_ref, last_t_ref, store):
    scale = rows_ref[1:2] if first_step else rows_ref[2:3]
    at = position("layer")
    odd = at % 2

    @pl.when((odd == 0) & (at > 0))
    def _():
        store(base_ref[...] + arrived_ref[...].astype(F32) * scale)

    @pl.when((odd == 1) & (at < count - 1))
    def _():
        store(base_ref[...] + product(arrived_ref[...], last_t_ref[...]) * scale)

    @pl.when((at == 0) | ((odd == 1) & (at == count - 1)))
    def _():
        store(base_ref[...])


def step_kernel(
    count, first_step, rows_ref, base_ref, arrived_ref, last_ref, last_t_ref, next_ref, next16_ref, send_ref
):
    def store(block):
        next_ref[...] = block
        next16_ref[...] = block.astype(BF16)

    finish(count, first_step, rows_ref, base_ref, arrived_ref, last_t_ref, store)
    send_outer(position("layer") % 2, next16_ref, last_ref, send_ref)


def last_kernel(
    count, rows_ref, base_ref, arrived_ref, last_t_ref, rest16_ref, rest_gram_ref,
    next_ref, next16_ref, low_ref, gram_ref,
):
    def store(block):
        next_ref[...] = block
        next16_ref[...] = block.astype(BF16)

    finish(count, False, rows_ref, base_ref, arrived_ref, last_t_ref, store)
    edge = low_ref.shape[1]
    low_ref[0] = next16_ref[:edge]
    for i in range(low_ref.shape[0] - 1):
        low_ref[i + 1] = rest16_ref[i, :edge]
    gram_ref[...] = rest_gram_ref[...] + product_t(next_ref[...], next_ref[...], HIGHEST)


def normal_kernel(parts, length, *refs):
    grams, (filtered_ref, last_ref, inverse_ref, outer_ref, outer16_ref, send_ref) = refs[:parts], refs[parts:]
    inverse_ref[...] = inverse_factor(sum(ref[...] for ref in grams) * (1.0 / length))
    outer_ref[...] = exact(inverse_ref[...], filtered_ref[...])
    outer16_ref[...] = outer_ref[...].astype(BF16)
    send_outer(position("layer") % 2, outer16_ref, last_ref, send_ref)


def normal_rest_kernel(inverse_ref, filtered_ref, last_ref, rest_ref, rest16_ref, send_ref):
    for i in range(rest_ref.shape[0]):
        rest_ref[i] = exact(inverse_ref[...], filtered_ref[i])
    rest16_ref[...] = rest_ref[...].astype(BF16)
    send_inner(position("layer") % 2, rest16_ref, last_ref, send_ref)


def cross_kernel(gram_ref, outer16_ref, rest16_ref, above_ref, out_ref):
    size, edge = gram_ref.shape[0], above_ref.shape[1]
    rest = range(rest16_ref.shape[0])
    out_ref[:, :size] = gram_ref[...]
    out_ref[:, size : size + edge] = product_t(outer16_ref[...], above_ref[0]) + sum(
        product_t(rest16_ref[i], above_ref[i + 1]) for i in rest
    )
    out_ref[:edge, size + edge :] = sum(
        product_t(above_ref[l], above_ref[l]) for l in range(above_ref.shape[0])
    )
    out_ref[edge:, size + edge :] = jnp.zeros((size - edge, edge), F32)


def factor_kernel(parts, length, slices, *refs):
    grams, (outer_ref, rest_ref, inverse_ref, weights_ref, up_ref) = refs[:parts], refs[parts:]
    size, edge = outer_ref.shape[0], up_ref.shape[1]
    total = sum(ref[...] for ref in grams) * (1.0 / length)
    has_above = (position("cuts") < slices - 1).astype(F32)
    row = lax.broadcasted_iota(jnp.int32, (edge, edge), 0)
    column = lax.broadcasted_iota(jnp.int32, (edge, edge), 1)
    identity = jnp.where(row == column, 1.0, 0.0)
    above_gram = total[:edge, size + edge :] * has_above + identity * (1.0 - has_above)
    own = inverse_factor(total[:, :size])
    above = inverse_factor(above_gram)
    inverse_ref[...] = own
    high = own[size - edge :]
    correlation = product_t(exact(high, total[:, size : size + edge]), above, HIGHEST) * has_above
    weights_ref[...] = exact(correlation, above)
    up = exact(correlation.T, high)
    up_ref[0] = exact(up, outer_ref[...]).astype(BF16)
    for i in range(rest_ref.shape[0]):
        up_ref[i + 1] = exact(up, rest_ref[i]).astype(BF16)


def final_kernel(slices, inverse_ref, weights_ref, outer_ref, rest_ref, above_ref, below_ref, out_ref):
    size, edge = outer_ref.shape[0], above_ref.shape[1]
    layers = above_ref.shape[0]
    has_below = (position("cuts") > 0).astype(F32)
    blocks = []
    for i in range(layers):
        block = exact(inverse_ref[...], rest_ref[i - 1] if i else outer_ref[...])
        high = block[size - edge :] - exact(weights_ref[...], above_ref[i].astype(F32))
        low = block[:edge] - below_ref[i].astype(F32) * has_below
        blocks.append(jnp.concatenate([low, block[edge : size - edge], high], 0))
    for parity in (0, 1):

        @pl.when(position("layer") % 2 == parity)
        def _():
            for i, l in enumerate(range(layers)[:: -1 if parity else 1]):
                out_ref[:, l, :] = blocks[i]


def per_device(vectors, diag_blocks, couplings, bounds):
    vectors = vectors[0]
    count_vec, layers, width = vectors.shape
    count, slices = lax.axis_size("layer"), lax.axis_size("cuts")
    length_all = count * layers * width

    def array(dtype, *shape):
        return jax.ShapeDtypeStruct(shape, dtype)

    outer32, outer16 = array(F32, count_vec, width), array(BF16, count_vec, width)
    rest32, rest16 = array(F32, layers - 1, count_vec, width), array(BF16, layers - 1, count_vec, width)
    square = array(F32, count_vec, count_vec)
    matrix = array(BF16, width, width)
    matrices = array(BF16, layers - 1, width, width)
    edges = array(BF16, layers, EDGE, width)
    one = 2 * count_vec * width * width

    def call(kernel, outs, *operands, far=(), scratch_shapes=(), flops=one):
        moved = sum(x.size * x.dtype.itemsize for x in operands)
        return pl.pallas_call(
            kernel,
            out_shape=outs,
            in_specs=[HBM if i in far else VMEM for i in range(len(operands))],
            out_specs=jax.tree.map(lambda _: VMEM, outs),
            scratch_shapes=list(scratch_shapes),
            compiler_params=pltpu.CompilerParams(vmem_limit_bytes=32 * 2**20),
            cost_estimate=pl.CostEstimate(flops=flops, bytes_accessed=moved, transcendentals=0),
        )(*operands)

    outer, rest, outer_r, rest_r, inner_send, outer_send, last, mids, rows = call(
        enter_kernel,
        (outer32, rest32, outer16, rest16, outer16, outer16, matrix, matrices, array(F32, 8, width)),
        *map(far_away, (bounds, vectors, couplings)), far=(0, 1, 2),
        scratch_shapes=[
            pltpu.SMEM(bounds.shape, jnp.int32),
            pltpu.VMEM(vectors.shape, F32),
            pltpu.SemaphoreType.DMA((4,)),
        ],
    )

    def filter_block(outer, rest, outer_r, rest_r, inner_send, outer_send, turned):
        outer_before, rest_before = outer, rest
        for step in range(DEG):
            final = step == DEG - 1
            outer_in = exchanged(outer_send, 1)
            inner_in = exchanged(inner_send, 0)
            load = not turned
            outs = (outer32, rest32, rest16, square if final else outer16)
            base, rest_next, rest_r, extra, *made = call(
                functools.partial(interior_kernel, layers, load, step == 0, final),
                outs + ((matrix, matrices) if load else ()),
                rows, outer_r, rest_r, inner_in, diag_blocks, last, mids, *turned,
                outer, rest, outer_before, rest_before,
                scratch_shapes=[pltpu.VMEM((count_vec, width), F32)],
                flops=(3 * layers - 1) * one,
            )
            turned = turned or made
            if final:
                outer_next, outer_r, low, gram = call(
                    functools.partial(last_kernel, count),
                    (outer32, outer16, edges, square),
                    rows, base, outer_in, turned[0], rest_r, extra,
                )
                return outer_next, rest_next, outer_r, rest_r, low, gram, turned
            inner_send = extra
            outer_next, outer_r, outer_send = call(
                functools.partial(step_kernel, count, step == 0),
                (outer32, outer16, outer16),
                rows, base, outer_in, last, turned[0],
            )
            outer_before, rest_before, outer, rest = outer, rest, outer_next, rest_next

    outer, rest, _, _, _, gram, turned = filter_block(
        outer, rest, outer_r, rest_r, inner_send, outer_send, []
    )
    grams = partial_sums(gram)
    inverse, outer, outer_r, outer_send = call(
        functools.partial(normal_kernel, len(grams), length_all),
        (square, outer32, outer16, outer16), *grams, outer, last,
    )
    rest, rest_r, inner_send = call(
        normal_rest_kernel, (rest32, rest16, outer16), inverse, rest, last
    )
    outer, rest, outer_r, rest_r, low, gram, _ = filter_block(
        outer, rest, outer_r, rest_r, inner_send, outer_send, turned
    )
    above = rotated(low, -1)
    cross = call(
        cross_kernel, array(F32, count_vec, count_vec + 2 * EDGE), gram, outer_r, rest_r, above
    )
    grams = partial_sums(cross)
    inverse, weights, up = call(
        functools.partial(factor_kernel, len(grams), length_all, slices),
        (square, array(F32, EDGE, EDGE), edges), *grams, outer, rest,
    )
    below = rotated(up, 1)
    result = call(
        functools.partial(final_kernel, slices),
        array(F32, count_vec, layers, width), inverse, weights, outer, rest, above, below,
    )
    return result[None]


def solution(mesh):
    in_specs = (
        P("cuts", None, "layer", None),
        P("layer", None, None),
        P("layer", None, None),
        P("cuts", None),
    )
    out_specs = P("cuts", None, "layer", None)
    return jax.shard_map(
        per_device, mesh=mesh, in_specs=in_specs, out_specs=out_specs, check_vma=False
    )
```

```python
import functools

import jax
import jax.numpy as jnp
from jax import lax
from jax.experimental import pallas as pl
from jax.experimental.pallas import tpu as pltpu
from jax.sharding import PartitionSpec as P

EDGE = 16
DEG = 4
STEPS = 2
ROWS = 8
HIGHEST = lax.Precision.HIGHEST
BF16 = jnp.bfloat16
F32 = jnp.float32
VMEM = pl.BlockSpec(memory_space=pltpu.VMEM)
HBM = pl.BlockSpec(memory_space=pltpu.HBM)


def exchanged(block, first):
    count, slices = lax.axis_size("layer"), lax.axis_size("cuts")
    route = []
    for cut in range(slices):
        for i in range(count):
            j = i + 1 if (i - first) % 2 == 0 else i - 1
            to = (cut, j) if 0 <= j < count else (cut ^ 1 if cut ^ 1 < slices else cut, i)
            route.append((cut * count + i, to[0] * count + to[1]))
    return lax.ppermute(block, ("cuts", "layer"), route)


def far_away(block):
    return pltpu.with_memory_space_constraint(block, pltpu.HBM)


def rotated(block, distance):
    size = lax.axis_size("cuts")
    return lax.ppermute(block, "cuts", [(i, (i + distance) % size) for i in range(size)])


def doublings():
    size = lax.axis_size("layer")
    return [] if size & (size - 1) else [1 << i for i in range(size.bit_length() - 1)]


def swapped(block, reach):
    return lax.ppermute(block, "layer", [(i, i ^ reach) for i in range(lax.axis_size("layer"))])


def partial_sums(block):
    size = lax.axis_size("layer")
    if not doublings():
        return [lax.psum(block, "layer")]
    reach = 1
    while size // reach > 4:
        block = block + swapped(block, reach)
        reach *= 2
    return [block] + [swapped(block, step) for step in range(reach, size, reach)]


def product(block, matrix):
    return jnp.dot(block, matrix, preferred_element_type=F32)


def product_t(block, matrix, precision=None):
    return lax.dot_general(
        block, matrix, (((1,), (1,)), ((), ())), precision=precision, preferred_element_type=F32
    )


def exact(first, second):
    return jnp.dot(first, second, precision=HIGHEST, preferred_element_type=F32)


def inverse_factor(gram):
    size = gram.shape[0]
    row = lax.broadcasted_iota(jnp.int32, (size, size), 0)
    column = lax.broadcasted_iota(jnp.int32, (size, size), 1)
    work = jnp.concatenate([jnp.where(row == column, 1.0, 0.0), gram], 1)
    finished = []
    for start in range(0, size, ROWS):
        left = size - start
        at = lax.broadcasted_iota(jnp.int32, (left, 2 * size), 0)
        lines = [
            jnp.broadcast_to(work[:, size + start + c : size + start + c + 1], (left, 2 * size))
            for c in range(ROWS)
        ]
        pivots = jnp.zeros((ROWS, 2 * size), F32)
        for c in range(ROWS):
            pivot = lines[c][c : c + 1]
            factor = jnp.where(at > c, lines[c] * (1.0 / pivot), 0.0)
            pivots = jnp.where(at[:ROWS] == c, pivot, pivots)
            work = work - factor * work[c : c + 1]
            for d in range(c + 1, ROWS):
                lines[d] = lines[d] - factor * lines[d][c : c + 1]
        finished.append(lax.rsqrt(pivots) * work[:ROWS])
        work = work[ROWS:]
    return jnp.concatenate(finished, 0)[:, :size]


def position(axis):
    return lax.axis_index(axis).astype(jnp.int32)


def send_outer(odd, rounded_ref, last_ref, send_ref):
    @pl.when(odd == 0)
    def _():
        send_ref[...] = rounded_ref[...]

    @pl.when(odd == 1)
    def _():
        send_ref[...] = product(rounded_ref[...], last_ref[...]).astype(BF16)


def send_inner(odd, rounded_ref, last_ref, send_ref):
    end = rounded_ref.shape[0] - 1

    @pl.when(odd == 1)
    def _():
        send_ref[...] = rounded_ref[end]

    @pl.when(odd == 0)
    def _():
        send_ref[...] = product(rounded_ref[end], last_ref[...]).astype(BF16)


def enter_kernel(
    far_bounds_ref, vectors_ref, couplings_ref,
    outer_ref, rest_ref, outer16_ref, rest16_ref, inner_send_ref, outer_send_ref, last_ref, mids_ref, rows_ref,
    bounds_ref, block_ref, sems,
):
    layers = vectors_ref.shape[1]
    copies = [
        pltpu.make_async_copy(vectors_ref, block_ref, sems.at[0]),
        pltpu.make_async_copy(couplings_ref.at[layers - 1], last_ref, sems.at[1]),
        pltpu.make_async_copy(couplings_ref.at[pl.ds(0, layers - 1)], mids_ref, sems.at[2]),
        pltpu.make_async_copy(far_bounds_ref, bounds_ref, sems.at[3]),
    ]
    for copy in copies:
        copy.start()
    odd = position("layer") % 2
    copies[0].wait()
    for parity in (0, 1):

        @pl.when(odd == parity)
        def _():
            order = range(layers)[:: -1 if parity else 1]
            outer_ref[...] = block_ref[:, order[0], :]
            for i, l in enumerate(order[1:]):
                rest_ref[i] = block_ref[:, l, :]

    outer16_ref[...] = outer_ref[...].astype(BF16)
    rest16_ref[...] = rest_ref[...].astype(BF16)
    copies[1].wait()
    send_outer(odd, outer16_ref, last_ref, outer_send_ref)
    send_inner(odd, rest16_ref, last_ref, inner_send_ref)
    copies[3].wait()
    width = rows_ref.shape[1]
    low, high = bounds_ref[0, 0].astype(F32), bounds_ref[0, 1].astype(F32)
    half = jnp.full((1, width), (high - low) * (1.0 / 128.0), F32)
    rows_ref[0:1] = jnp.full((1, width), (low + high) * (1.0 / 128.0), F32)
    rows_ref[1:2] = 1.0 / half
    rows_ref[2:3] = 2.0 / half
    copies[2].wait()


def interior_kernel(
    layers, load, first_step, gram, adds, final, rows_ref, outer16_ref, rest16_ref, arrived_ref, diag_ref, last_ref, mids_ref, *refs,
):
    *refs, sum_ref = refs
    if load:
        (outer_ref, rest_ref, outer_before_ref, rest_before_ref, *outs, last_t_ref, mids_t_ref) = refs
        last_t_ref[...] = jnp.transpose(last_ref[...])
        for i in range(layers - 1):
            mids_t_ref[i] = jnp.transpose(mids_ref[i])
    else:
        (last_t_ref, mids_t_ref, outer_ref, rest_ref, outer_before_ref, rest_before_ref, *outs) = refs
    if adds:
        here_ref, there_ref, *outs, total_ref = outs
        total_ref[...] = here_ref[...] + there_ref[...]
    base_ref, next_ref, next16_ref, *outs = outs
    centre, scale = rows_ref[0:1], rows_ref[1:2] if first_step else rows_ref[2:3]
    odd = position("layer") % 2

    def rounded(place):
        return rest16_ref[place - 1] if place else outer16_ref[...]

    def add(block, straight, link):
        @pl.when(odd == straight)
        def _():
            sum_ref[...] += product(block, mids_ref[link])

        @pl.when(odd != straight)
        def _():
            sum_ref[...] += product(block, mids_t_ref[link])

    for place in range(layers)[::-1]:
        sum_ref[...] = product(rounded(place), diag_ref[place + odd * (layers - 1 - 2 * place)])
        if place < layers - 1:
            add(rounded(place + 1), 1, place + odd * (layers - 2 - 2 * place))
        if place > 0:
            add(rounded(place - 1), 0, place - 1 + odd * (layers - 2 * place))
        if place == layers - 1:

            @pl.when(odd == 0)
            def _():
                sum_ref[...] += product(arrived_ref[...], last_t_ref[...])

            @pl.when(odd == 1)
            def _():
                sum_ref[...] += arrived_ref[...].astype(F32)

        if place:
            term = (sum_ref[...] - centre * rest_ref[place - 1]) * scale
            term = term if first_step else term - rest_before_ref[place - 1]
            next_ref[place - 1] = term
            next16_ref[place - 1] = term.astype(BF16)
        else:
            term = (sum_ref[...] - centre * outer_ref[...]) * scale
            base_ref[...] = term if first_step else term - outer_before_ref[...]
    if not final:
        send_inner(odd, next16_ref, last_ref, outs[0])
    if gram:
        outs[1][...] = product_t(outer_ref[...], outer_ref[...], HIGHEST) + sum(
            product_t(rest_ref[i], rest_ref[i], HIGHEST) for i in range(layers - 1)
        )


def finish(count, first_step, rows_ref, base_ref, arrived_ref, last_t_ref, store):
    scale = rows_ref[1:2] if first_step else rows_ref[2:3]
    at = position("layer")
    odd = at % 2

    @pl.when((odd == 0) & (at > 0))
    def _():
        store(base_ref[...] + arrived_ref[...].astype(F32) * scale)

    @pl.when((odd == 1) & (at < count - 1))
    def _():
        store(base_ref[...] + product(arrived_ref[...], last_t_ref[...]) * scale)

    @pl.when((at == 0) | ((odd == 1) & (at == count - 1)))
    def _():
        store(base_ref[...])


def step_kernel(
    count, first_step, rows_ref, base_ref, arrived_ref, last_ref, last_t_ref, next_ref, next16_ref, send_ref
):
    def store(block):
        next_ref[...] = block
        next16_ref[...] = block.astype(BF16)

    finish(count, first_step, rows_ref, base_ref, arrived_ref, last_t_ref, store)
    send_outer(position("layer") % 2, next16_ref, last_ref, send_ref)


def normal_kernel(parts, length, *refs):
    grams, (rest_ref, inverse_ref, next_ref, next16_ref, gram_ref) = refs[:parts], refs[parts:]
    inverse_ref[...] = inverse_factor(sum(ref[...] for ref in grams) * (1.0 / length))
    gram_ref[...] = jnp.zeros(gram_ref.shape, F32)
    for i in range(rest_ref.shape[0]):
        block = exact(inverse_ref[...], rest_ref[i])
        next_ref[i] = block
        next16_ref[i] = block.astype(BF16)
        gram_ref[...] += product_t(block, block, HIGHEST)


def last_kernel(
    count, rows_ref, base_ref, arrived_ref, last_t_ref, inverse_ref, rest16_ref, rest_gram_ref,
    next_ref, next16_ref, low_ref, gram_ref,
):
    def store(block):
        next_ref[...] = exact(inverse_ref[...], block)

    finish(count, False, rows_ref, base_ref, arrived_ref, last_t_ref, store)
    next16_ref[...] = next_ref[...].astype(BF16)
    edge = low_ref.shape[1]
    low_ref[0] = next16_ref[:edge]
    for i in range(low_ref.shape[0] - 1):
        low_ref[i + 1] = rest16_ref[i, :edge]
    gram_ref[...] = rest_gram_ref[...] + product_t(next_ref[...], next_ref[...], HIGHEST)


def cross_kernel(gram_ref, outer16_ref, rest16_ref, above_ref, out_ref):
    size, edge = gram_ref.shape[0], above_ref.shape[1]
    rest = range(rest16_ref.shape[0])
    out_ref[:, :size] = gram_ref[...]
    out_ref[:, size : size + edge] = product_t(outer16_ref[...], above_ref[0]) + sum(
        product_t(rest16_ref[i], above_ref[i + 1]) for i in rest
    )
    out_ref[:edge, size + edge :] = sum(
        product_t(above_ref[l], above_ref[l]) for l in range(above_ref.shape[0])
    )
    out_ref[edge:, size + edge :] = jnp.zeros((size - edge, edge), F32)


def factor_kernel(parts, length, slices, *refs):
    grams, (outer_ref, rest_ref, inverse_ref, weights_ref, up_ref) = refs[:parts], refs[parts:]
    size, edge = outer_ref.shape[0], up_ref.shape[1]
    total = sum(ref[...] for ref in grams) * (1.0 / length)
    has_above = (position("cuts") < slices - 1).astype(F32)
    row = lax.broadcasted_iota(jnp.int32, (edge, edge), 0)
    column = lax.broadcasted_iota(jnp.int32, (edge, edge), 1)
    identity = jnp.where(row == column, 1.0, 0.0)
    above_gram = total[:edge, size + edge :] * has_above + identity * (1.0 - has_above)
    own = inverse_factor(total[:, :size])
    above = inverse_factor(above_gram)
    inverse_ref[...] = own
    high = own[size - edge :]
    correlation = product_t(exact(high, total[:, size : size + edge]), above, HIGHEST) * has_above
    weights_ref[...] = exact(correlation, above)
    up = exact(correlation.T, high)
    up_ref[0] = exact(up, outer_ref[...]).astype(BF16)
    for i in range(rest_ref.shape[0]):
        up_ref[i + 1] = exact(up, rest_ref[i]).astype(BF16)


def final_kernel(slices, inverse_ref, weights_ref, outer_ref, rest_ref, above_ref, below_ref, out_ref):
    size, edge = outer_ref.shape[0], above_ref.shape[1]
    layers = above_ref.shape[0]
    has_below = (position("cuts") > 0).astype(F32)
    blocks = []
    for i in range(layers):
        block = exact(inverse_ref[...], rest_ref[i - 1] if i else outer_ref[...])
        high = block[size - edge :] - exact(weights_ref[...], above_ref[i].astype(F32))
        low = block[:edge] - below_ref[i].astype(F32) * has_below
        blocks.append(jnp.concatenate([low, block[edge : size - edge], high], 0))
    for parity in (0, 1):

        @pl.when(position("layer") % 2 == parity)
        def _():
            for i, l in enumerate(range(layers)[:: -1 if parity else 1]):
                out_ref[:, l, :] = blocks[i]


def per_device(vectors, diag_blocks, couplings, bounds):
    vectors = vectors[0]
    count_vec, layers, width = vectors.shape
    count, slices = lax.axis_size("layer"), lax.axis_size("cuts")
    length_all = count * layers * width

    def array(dtype, *shape):
        return jax.ShapeDtypeStruct(shape, dtype)

    outer32, outer16 = array(F32, count_vec, width), array(BF16, count_vec, width)
    rest32, rest16 = array(F32, layers - 1, count_vec, width), array(BF16, layers - 1, count_vec, width)
    square = array(F32, count_vec, count_vec)
    matrix = array(BF16, width, width)
    matrices = array(BF16, layers - 1, width, width)
    edges = array(BF16, layers, EDGE, width)
    one = 2 * count_vec * width * width

    def call(kernel, outs, *operands, far=(), scratch_shapes=(), flops=one):
        moved = sum(x.size * x.dtype.itemsize for x in operands)
        return pl.pallas_call(
            kernel,
            out_shape=outs,
            in_specs=[HBM if i in far else VMEM for i in range(len(operands))],
            out_specs=jax.tree.map(lambda _: VMEM, outs),
            scratch_shapes=list(scratch_shapes),
            compiler_params=pltpu.CompilerParams(vmem_limit_bytes=32 * 2**20),
            cost_estimate=pl.CostEstimate(flops=flops, bytes_accessed=moved, transcendentals=0),
        )(*operands)

    outer, rest, outer_r, rest_r, inner_send, outer_send, last, mids, rows = call(
        enter_kernel,
        (outer32, rest32, outer16, rest16, outer16, outer16, matrix, matrices, array(F32, 8, width)),
        *map(far_away, (bounds, vectors, couplings)), far=(0, 1, 2),
        scratch_shapes=[
            pltpu.SMEM(bounds.shape, jnp.int32),
            pltpu.VMEM(vectors.shape, F32),
            pltpu.SemaphoreType.DMA((4,)),
        ],
    )

    outer_before, rest_before = outer, rest
    turned, reaches = [], doublings()
    applications = STEPS * DEG
    for step in range(applications):
        first_step, final, gram = step % DEG == 0, step == applications - 1, step == DEG
        load = step == 0
        outer_in = exchanged(outer_send, 1)
        inner_in = exchanged(inner_send, 0)
        adds = step > DEG and bool(reaches) and not final
        base, rest_next, rest_r, *extra = call(
            functools.partial(interior_kernel, layers, load, first_step, gram, adds, final),
            (outer32, rest32, rest16)
            + (() if final else (outer16,))
            + ((square,) if gram or adds else ())
            + ((matrix, matrices) if load else ()),
            rows, outer_r, rest_r, inner_in, diag_blocks, last, mids, *turned,
            outer, rest, outer_before, rest_before,
            *((total, swapped(total, reaches.pop(0))) if adds else ()),
            scratch_shapes=[pltpu.VMEM((count_vec, width), F32)],
            flops=(3 * layers - 1) * one,
        )
        if load:
            *extra, last_t, mids_t = extra
            turned = [last_t, mids_t]
        if gram or adds:
            total = extra[-1]
        if gram and not reaches:
            total = lax.psum(total, "layer")
        if final:
            break
        outer_next, outer_r, outer_send = call(
            functools.partial(step_kernel, count, first_step),
            (outer32, outer16, outer16), rows, base, outer_in, last, last_t,
        )
        inner_send = extra[0]
        outer_before, rest_before, outer, rest = outer, rest, outer_next, rest_next

    totals = [total]
    for reach in reaches:
        totals = [sum(totals), swapped(sum(totals), reach)]
    inverse, rest, rest_r, rest_gram = call(
        functools.partial(normal_kernel, len(totals), length_all),
        (square, rest32, rest16, square), *totals, rest_next,
    )
    outer, outer_r, low, gram = call(
        functools.partial(last_kernel, count), (outer32, outer16, edges, square),
        rows, base, outer_in, last_t, inverse, rest_r, rest_gram,
    )
    above = rotated(low, -1)
    cross = call(
        cross_kernel, array(F32, count_vec, count_vec + 2 * EDGE), gram, outer_r, rest_r, above
    )
    grams = partial_sums(cross)
    inverse, weights, up = call(
        functools.partial(factor_kernel, len(grams), length_all, slices),
        (square, array(F32, EDGE, EDGE), edges), *grams, outer, rest,
    )
    below = rotated(up, 1)
    result = call(
        functools.partial(final_kernel, slices),
        array(F32, count_vec, layers, width), inverse, weights, outer, rest, above, below,
    )
    return result[None]


def solution(mesh):
    in_specs = (
        P("cuts", None, "layer", None),
        P("layer", None, None),
        P("layer", None, None),
        P("cuts", None),
    )
    out_specs = P("cuts", None, "layer", None)
    return jax.shard_map(
        per_device, mesh=mesh, in_specs=in_specs, out_specs=out_specs, check_vma=False
    )
```

```python
import functools

import jax
import jax.numpy as jnp
from jax import lax
from jax.experimental import pallas as pl
from jax.experimental.pallas import tpu as pltpu
from jax.sharding import PartitionSpec as P

EDGE = 16
DEG = 4
STEPS = 2
ROWS = 8
HIGHEST = lax.Precision.HIGHEST
BF16 = jnp.bfloat16
F32 = jnp.float32
VMEM = pl.BlockSpec(memory_space=pltpu.VMEM)
HBM = pl.BlockSpec(memory_space=pltpu.HBM)


def exchanged(block, first):
    count, slices = lax.axis_size("layer"), lax.axis_size("cuts")
    route = []
    for cut in range(slices):
        for i in range(count):
            j = i + 1 if (i - first) % 2 == 0 else i - 1
            to = (cut, j) if 0 <= j < count else (cut ^ 1 if cut ^ 1 < slices else cut, i)
            route.append((cut * count + i, to[0] * count + to[1]))
    return lax.ppermute(block, ("cuts", "layer"), route)


def far_away(block):
    return pltpu.with_memory_space_constraint(block, pltpu.HBM)


def rotated(block, distance):
    size = lax.axis_size("cuts")
    return lax.ppermute(block, "cuts", [(i, (i + distance) % size) for i in range(size)])


def doublings():
    size = lax.axis_size("layer")
    return [] if size & (size - 1) else [1 << i for i in range(size.bit_length() - 1)]


def swapped(block, reach):
    far = reach | 1
    return lax.ppermute(block, "layer", [(i, i ^ far) for i in range(lax.axis_size("layer"))])


def partial_sums(block):
    size = lax.axis_size("layer")
    if not doublings():
        return [lax.psum(block, "layer")]
    reach = 1
    while size // reach > 4:
        block = block + swapped(block, reach)
        reach *= 2
    return [block] + [swapped(block, step) for step in range(reach, size, reach)]


def product(block, matrix):
    return jnp.dot(block, matrix, preferred_element_type=F32)


def product_t(block, matrix, precision=None):
    return lax.dot_general(
        block, matrix, (((1,), (1,)), ((), ())), precision=precision, preferred_element_type=F32
    )


def exact(first, second):
    return jnp.dot(first, second, precision=HIGHEST, preferred_element_type=F32)


def inverse_factor(gram):
    size = gram.shape[0]
    row = lax.broadcasted_iota(jnp.int32, (size, size), 0)
    column = lax.broadcasted_iota(jnp.int32, (size, size), 1)
    work = jnp.concatenate([jnp.where(row == column, 1.0, 0.0), gram], 1)
    finished = []
    for start in range(0, size, ROWS):
        left = size - start
        at = lax.broadcasted_iota(jnp.int32, (left, 2 * size), 0)
        lines = [
            jnp.broadcast_to(work[:, size + start + c : size + start + c + 1], (left, 2 * size))
            for c in range(ROWS)
        ]
        pivots = jnp.zeros((ROWS, 2 * size), F32)
        for c in range(ROWS):
            pivot = lines[c][c : c + 1]
            factor = jnp.where(at > c, lines[c] * (1.0 / pivot), 0.0)
            pivots = jnp.where(at[:ROWS] == c, pivot, pivots)
            work = work - factor * work[c : c + 1]
            for d in range(c + 1, ROWS):
                lines[d] = lines[d] - factor * lines[d][c : c + 1]
        finished.append(lax.rsqrt(pivots) * work[:ROWS])
        work = work[ROWS:]
    return jnp.concatenate(finished, 0)[:, :size]


def position(axis):
    return lax.axis_index(axis).astype(jnp.int32)


def send_outer(odd, rounded_ref, last_ref, send_ref):
    @pl.when(odd == 0)
    def _():
        send_ref[...] = rounded_ref[...]

    @pl.when(odd == 1)
    def _():
        send_ref[...] = product(rounded_ref[...], last_ref[...]).astype(BF16)


def send_inner(odd, rounded_ref, last_ref, send_ref):
    end = rounded_ref.shape[0] - 1

    @pl.when(odd == 1)
    def _():
        send_ref[...] = rounded_ref[end]

    @pl.when(odd == 0)
    def _():
        send_ref[...] = product(rounded_ref[end], last_ref[...]).astype(BF16)


def enter_kernel(
    far_bounds_ref, vectors_ref, couplings_ref,
    outer_ref, rest_ref, outer16_ref, rest16_ref, inner_send_ref, outer_send_ref, last_ref, mids_ref, rows_ref,
    bounds_ref, block_ref, sems,
):
    layers = vectors_ref.shape[1]
    copies = [
        pltpu.make_async_copy(vectors_ref, block_ref, sems.at[0]),
        pltpu.make_async_copy(couplings_ref.at[layers - 1], last_ref, sems.at[1]),
        pltpu.make_async_copy(couplings_ref.at[pl.ds(0, layers - 1)], mids_ref, sems.at[2]),
        pltpu.make_async_copy(far_bounds_ref, bounds_ref, sems.at[3]),
    ]
    for copy in copies:
        copy.start()
    odd = position("layer") % 2
    copies[0].wait()
    for parity in (0, 1):

        @pl.when(odd == parity)
        def _():
            order = range(layers)[:: -1 if parity else 1]
            outer_ref[...] = block_ref[:, order[0], :]
            for i, l in enumerate(order[1:]):
                rest_ref[i] = block_ref[:, l, :]

    outer16_ref[...] = outer_ref[...].astype(BF16)
    rest16_ref[...] = rest_ref[...].astype(BF16)
    copies[1].wait()
    send_outer(odd, outer16_ref, last_ref, outer_send_ref)
    send_inner(odd, rest16_ref, last_ref, inner_send_ref)
    copies[3].wait()
    width = rows_ref.shape[1]
    low, high = bounds_ref[0, 0].astype(F32), bounds_ref[0, 1].astype(F32)
    half = jnp.full((1, width), (high - low) * (1.0 / 128.0), F32)
    rows_ref[0:1] = jnp.full((1, width), (low + high) * (1.0 / 128.0), F32)
    rows_ref[1:2] = 1.0 / half
    rows_ref[2:3] = 2.0 / half
    copies[2].wait()


def interior_kernel(
    layers, load, first_step, gram, adds, final, rows_ref, outer16_ref, rest16_ref, arrived_ref, diag_ref, last_ref, mids_ref, *refs,
):
    *refs, sum_ref = refs
    if load:
        (outer_ref, rest_ref, outer_before_ref, rest_before_ref, *outs, last_t_ref, mids_t_ref) = refs
        last_t_ref[...] = jnp.transpose(last_ref[...])
        for i in range(layers - 1):
            mids_t_ref[i] = jnp.transpose(mids_ref[i])
    else:
        (last_t_ref, mids_t_ref, outer_ref, rest_ref, outer_before_ref, rest_before_ref, *outs) = refs
    if adds:
        here_ref, there_ref, *outs, total_ref = outs
        total_ref[...] = here_ref[...] + there_ref[...]
    base_ref, next_ref, next16_ref, *outs = outs
    centre, scale = rows_ref[0:1], rows_ref[1:2] if first_step else rows_ref[2:3]
    odd = position("layer") % 2

    def rounded(place):
        return rest16_ref[place - 1] if place else outer16_ref[...]

    def add(block, straight, link):
        @pl.when(odd == straight)
        def _():
            sum_ref[...] += product(block, mids_ref[link])

        @pl.when(odd != straight)
        def _():
            sum_ref[...] += product(block, mids_t_ref[link])

    for place in range(layers)[::-1]:
        sum_ref[...] = product(rounded(place), diag_ref[place + odd * (layers - 1 - 2 * place)])
        if place < layers - 1:
            add(rounded(place + 1), 1, place + odd * (layers - 2 - 2 * place))
        if place > 0:
            add(rounded(place - 1), 0, place - 1 + odd * (layers - 2 * place))
        if place == layers - 1:

            @pl.when(odd == 0)
            def _():
                sum_ref[...] += product(arrived_ref[...], last_t_ref[...])

            @pl.when(odd == 1)
            def _():
                sum_ref[...] += arrived_ref[...].astype(F32)

        if place:
            term = (sum_ref[...] - centre * rest_ref[place - 1]) * scale
            term = term if first_step else term - rest_before_ref[place - 1]
            next_ref[place - 1] = term
            next16_ref[place - 1] = term.astype(BF16)
        else:
            term = (sum_ref[...] - centre * outer_ref[...]) * scale
            base_ref[...] = term if first_step else term - outer_before_ref[...]
    if not final:
        send_inner(odd, next16_ref, last_ref, outs[0])
    if gram:
        outs[1][...] = product_t(outer_ref[...], outer_ref[...], HIGHEST) + sum(
            product_t(rest_ref[i], rest_ref[i], HIGHEST) for i in range(layers - 1)
        )


def finish(count, first_step, rows_ref, base_ref, arrived_ref, last_t_ref, store):
    scale = rows_ref[1:2] if first_step else rows_ref[2:3]
    at = position("layer")
    odd = at % 2

    @pl.when((odd == 0) & (at > 0))
    def _():
        store(base_ref[...] + arrived_ref[...].astype(F32) * scale)

    @pl.when((odd == 1) & (at < count - 1))
    def _():
        store(base_ref[...] + product(arrived_ref[...], last_t_ref[...]) * scale)

    @pl.when((at == 0) | ((odd == 1) & (at == count - 1)))
    def _():
        store(base_ref[...])


def step_kernel(
    count, first_step, rows_ref, base_ref, arrived_ref, last_ref, last_t_ref, next_ref, next16_ref, send_ref
):
    def store(block):
        next_ref[...] = block
        next16_ref[...] = block.astype(BF16)

    finish(count, first_step, rows_ref, base_ref, arrived_ref, last_t_ref, store)
    send_outer(position("layer") % 2, next16_ref, last_ref, send_ref)


def identity(size):
    row = lax.broadcasted_iota(jnp.int32, (size, size), 0)
    column = lax.broadcasted_iota(jnp.int32, (size, size), 1)
    return jnp.where(row == column, 1.0, 0.0)


def row_scales(gram):
    return lax.rsqrt(jnp.sum(gram * identity(gram.shape[0]), axis=1, keepdims=True))


def scale_kernel(parts, length, *refs):
    grams, (rest_ref, next_ref, next16_ref, gram_ref, scales_ref) = refs[:parts], refs[parts:]
    scales = row_scales(sum(ref[...] for ref in grams) * (1.0 / length))
    scales_ref[...] = jnp.broadcast_to(scales, scales_ref.shape)
    gram_ref[...] = jnp.zeros(gram_ref.shape, F32)
    for i in range(rest_ref.shape[0]):
        block = rest_ref[i] * scales
        next_ref[i] = block
        next16_ref[i] = block.astype(BF16)
        gram_ref[...] += product_t(block, block, HIGHEST)


def last_kernel(
    count, rows_ref, base_ref, arrived_ref, last_t_ref, scales_ref, rest16_ref, rest_gram_ref,
    next_ref, next16_ref, low_ref, gram_ref,
):
    def store(block):
        next_ref[...] = block * scales_ref[:, :1]

    finish(count, False, rows_ref, base_ref, arrived_ref, last_t_ref, store)
    next16_ref[...] = next_ref[...].astype(BF16)
    edge = low_ref.shape[1]
    low_ref[0] = next16_ref[:edge]
    for i in range(low_ref.shape[0] - 1):
        low_ref[i + 1] = rest16_ref[i, :edge]
    gram_ref[...] = rest_gram_ref[...] + product_t(next_ref[...], next_ref[...], HIGHEST)


def first_factor_kernel(parts, length, *refs):
    grams, (_, inverse_ref) = refs[:parts], refs[parts:]
    gram = sum(ref[...] for ref in grams) * (1.0 / length)
    scales = row_scales(gram)
    across = jnp.sum(identity(gram.shape[0]) * scales, axis=0, keepdims=True)
    inverse_ref[...] = inverse_factor(gram * scales * across)


def cross_kernel(gram_ref, outer16_ref, rest16_ref, above_ref, out_ref):
    size, edge = outer16_ref.shape[0], above_ref.shape[1]
    rest = range(rest16_ref.shape[0])
    out_ref[:, :size] = gram_ref[...]
    out_ref[:, size : size + edge] = product_t(outer16_ref[...], above_ref[0]) + sum(
        product_t(rest16_ref[i], above_ref[i + 1]) for i in rest
    )
    out_ref[:edge, size + edge :] = sum(
        product_t(above_ref[l], above_ref[l]) for l in range(above_ref.shape[0])
    )
    out_ref[edge:, size + edge :] = jnp.zeros((size - edge, edge), F32)


def factor_kernel(parts, length, slices, *refs):
    grams, (first_ref, outer_ref, rest_ref, inverse_ref, weights_ref, up_ref) = refs[:parts], refs[parts:]
    size, edge = outer_ref.shape[0], up_ref.shape[1]
    first = first_ref[...]
    total = sum(ref[...] for ref in grams) * (1.0 / length)
    has_above = (position("cuts") < slices - 1).astype(F32)
    above = total[:edge, size + edge :] * has_above + identity(edge) * (1.0 - has_above)
    above = inverse_factor(above)
    own = product_t(exact(first, total[:, :size]), first, HIGHEST)
    own = exact(inverse_factor(own), first)
    inverse_ref[...] = own
    high = own[size - edge :]
    correlation = product_t(exact(high, total[:, size : size + edge]), above, HIGHEST) * has_above
    up = exact(correlation.T, high)
    up_ref[0] = exact(up, outer_ref[...]).astype(BF16)
    for i in range(rest_ref.shape[0]):
        up_ref[i + 1] = exact(up, rest_ref[i]).astype(BF16)
    weights_ref[...] = exact(correlation, above)


def vectors_kernel(inverse_ref, weights_ref, outer_ref, rest_ref, above_ref, all_ref):
    layers, size, _ = all_ref.shape
    edge = above_ref.shape[1]
    for i in range(layers):
        block = exact(inverse_ref[...], rest_ref[i - 1] if i else outer_ref[...])
        all_ref[i] = block
        all_ref[i, size - edge :] = block[size - edge :] - exact(
            weights_ref[...], above_ref[i].astype(F32)
        )


def final_kernel(all_ref, below_ref, out_ref):
    layers, size, _ = all_ref.shape
    edge = below_ref.shape[1]
    has_below = (position("cuts") > 0).astype(F32)
    for parity in (0, 1):

        @pl.when(position("layer") % 2 == parity)
        def _():
            for i, l in enumerate(range(layers)[:: -1 if parity else 1]):
                out_ref[:edge, l, :] = all_ref[i, :edge] - below_ref[i].astype(F32) * has_below
                out_ref[edge:, l, :] = all_ref[i, edge:]


def per_device(vectors, diag_blocks, couplings, bounds):
    vectors = vectors[0]
    count_vec, layers, width = vectors.shape
    count, slices = lax.axis_size("layer"), lax.axis_size("cuts")
    length_all = count * layers * width

    def array(dtype, *shape):
        return jax.ShapeDtypeStruct(shape, dtype)

    outer32, outer16 = array(F32, count_vec, width), array(BF16, count_vec, width)
    rest32, rest16 = array(F32, layers - 1, count_vec, width), array(BF16, layers - 1, count_vec, width)
    square = array(F32, count_vec, count_vec)
    matrix = array(BF16, width, width)
    matrices = array(BF16, layers - 1, width, width)
    edges = array(BF16, layers, EDGE, width)
    one = 2 * count_vec * width * width

    def call(kernel, outs, *operands, far=(), scratch_shapes=(), flops=one):
        moved = sum(x.size * x.dtype.itemsize for x in operands)
        return pl.pallas_call(
            kernel,
            out_shape=outs,
            in_specs=[HBM if i in far else VMEM for i in range(len(operands))],
            out_specs=jax.tree.map(lambda _: VMEM, outs),
            scratch_shapes=list(scratch_shapes),
            compiler_params=pltpu.CompilerParams(vmem_limit_bytes=32 * 2**20),
            cost_estimate=pl.CostEstimate(flops=flops, bytes_accessed=moved, transcendentals=0),
        )(*operands)

    outer, rest, outer_r, rest_r, inner_send, outer_send, last, mids, rows = call(
        enter_kernel,
        (outer32, rest32, outer16, rest16, outer16, outer16, matrix, matrices, array(F32, 8, width)),
        *map(far_away, (bounds, vectors, couplings)), far=(0, 1, 2),
        scratch_shapes=[
            pltpu.SMEM(bounds.shape, jnp.int32),
            pltpu.VMEM(vectors.shape, F32),
            pltpu.SemaphoreType.DMA((4,)),
        ],
    )

    outer_before, rest_before = outer, rest
    turned, reaches = [], doublings()
    applications = STEPS * DEG
    for step in range(applications):
        first_step, final, gram = step % DEG == 0, step == applications - 1, step == DEG
        load = step == 0
        outer_in = exchanged(outer_send, 1)
        inner_in = exchanged(inner_send, 0)
        adds = step > DEG and bool(reaches) and not final
        base, rest_next, rest_r, *extra = call(
            functools.partial(interior_kernel, layers, load, first_step, gram, adds, final),
            (outer32, rest32, rest16)
            + (() if final else (outer16,))
            + ((square,) if gram or adds else ())
            + ((matrix, matrices) if load else ()),
            rows, outer_r, rest_r, inner_in, diag_blocks, last, mids, *turned,
            outer, rest, outer_before, rest_before,
            *((total, swapped(total, reaches.pop(0))) if adds else ()),
            scratch_shapes=[pltpu.VMEM((count_vec, width), F32)],
            flops=(3 * layers - 1) * one,
        )
        if load:
            *extra, last_t, mids_t = extra
            turned = [last_t, mids_t]
        if gram or adds:
            total = extra[-1]
        if gram and not reaches:
            total = lax.psum(total, "layer")
        if final:
            break
        outer_next, outer_r, outer_send = call(
            functools.partial(step_kernel, count, first_step),
            (outer32, outer16, outer16), rows, base, outer_in, last, last_t,
        )
        inner_send = extra[0]
        outer_before, rest_before, outer, rest = outer, rest, outer_next, rest_next

    totals = [total]
    for reach in reaches:
        totals = [sum(totals), swapped(sum(totals), reach)]
    rest, rest_r, rest_gram, scales = call(
        functools.partial(scale_kernel, len(totals), length_all),
        (rest32, rest16, square, array(F32, count_vec, 128)), *totals, rest_next,
    )
    outer, outer_r, low, gram = call(
        functools.partial(last_kernel, count), (outer32, outer16, edges, square),
        rows, base, outer_in, last_t, scales, rest_r, rest_gram,
    )
    above = rotated(low, -1)
    first = call(
        functools.partial(first_factor_kernel, len(totals), length_all), square, *totals, gram
    )
    cross = call(
        cross_kernel, array(F32, count_vec, count_vec + 2 * EDGE), gram, outer_r, rest_r, above
    )
    grams = partial_sums(cross)
    inverse, weights, up = call(
        functools.partial(factor_kernel, len(grams), length_all, slices),
        (square, array(F32, EDGE, EDGE), edges), *grams, first, outer, rest,
    )
    below = rotated(up, 1)
    vectors_all = call(
        vectors_kernel, array(F32, layers, count_vec, width), inverse, weights, outer, rest, above
    )
    result = call(final_kernel, array(F32, count_vec, layers, width), vectors_all, below)
    return result[None]


def solution(mesh):
    in_specs = (
        P("cuts", None, "layer", None),
        P("layer", None, None),
        P("layer", None, None),
        P("cuts", None),
    )
    out_specs = P("cuts", None, "layer", None)
    return jax.shard_map(
        per_device, mesh=mesh, in_specs=in_specs, out_specs=out_specs, check_vma=False
    )
```

```python
import functools

import jax
import jax.numpy as jnp
from jax import lax
from jax.experimental import pallas as pl
from jax.experimental.pallas import tpu as pltpu
from jax.sharding import PartitionSpec as P

EDGE = 16
DEG = 4
STEPS = 2
ROWS = 16
ROWS_FULL = 128
HIGHEST = lax.Precision.HIGHEST
BF16 = jnp.bfloat16
F32 = jnp.float32
VMEM = pl.BlockSpec(memory_space=pltpu.VMEM)
HBM = pl.BlockSpec(memory_space=pltpu.HBM)


def exchanged(block, first):
    count, slices = lax.axis_size("layer"), lax.axis_size("cuts")
    route = []
    for cut in range(slices):
        for i in range(count):
            j = i + 1 if (i - first) % 2 == 0 else i - 1
            to = (cut, j) if 0 <= j < count else (cut ^ 1 if cut ^ 1 < slices else cut, i)
            route.append((cut * count + i, to[0] * count + to[1]))
    return lax.ppermute(block, ("cuts", "layer"), route)


def far_away(block):
    return pltpu.with_memory_space_constraint(block, pltpu.HBM)


def rotated(block, distance):
    size = lax.axis_size("cuts")
    return lax.ppermute(block, "cuts", [(i, (i + distance) % size) for i in range(size)])


def doublings():
    size = lax.axis_size("layer")
    return [] if size & (size - 1) else [1 << i for i in range(size.bit_length() - 1)]


def swapped(block, reach):
    far = reach | 1
    return lax.ppermute(block, "layer", [(i, i ^ far) for i in range(lax.axis_size("layer"))])


def partial_sums(block):
    size = lax.axis_size("layer")
    if not doublings():
        return [lax.psum(block, "layer")]
    reach = 1
    while size // reach > 4:
        block = block + swapped(block, reach)
        reach *= 2
    return [block] + [swapped(block, step) for step in range(reach, size, reach)]


def product(block, matrix):
    size = block.shape[0]
    block = jnp.concatenate([block] * max(1, ROWS_FULL // size), 0)
    return jnp.dot(block, matrix, preferred_element_type=F32)[:size]


def product_t(block, matrix, precision=None):
    return lax.dot_general(
        block, matrix, (((1,), (1,)), ((), ())), precision=precision, preferred_element_type=F32
    )


def exact(first, second):
    return jnp.dot(first, second, precision=HIGHEST, preferred_element_type=F32)


def identity(size):
    row = lax.broadcasted_iota(jnp.int32, (size, size), 0)
    column = lax.broadcasted_iota(jnp.int32, (size, size), 1)
    return jnp.where(row == column, 1.0, 0.0)


def inverse_factors(*grams):
    sizes = [gram.shape[0] for gram in grams]
    works = [jnp.concatenate([identity(gram.shape[0]), gram], 1) for gram in grams]
    finished = [[] for _ in grams]
    for start in range(0, max(sizes), ROWS):
        live = [i for i, size in enumerate(sizes) if start < size]
        shapes = {i: (sizes[i] - start, 2 * sizes[i]) for i in live}
        at = {i: lax.broadcasted_iota(jnp.int32, shapes[i], 0) for i in live}
        lines, pivots = {}, {}
        for i in live:
            first = sizes[i] + start
            lines[i] = [
                jnp.broadcast_to(works[i][:, first + c : first + c + 1], shapes[i])
                for c in range(ROWS)
            ]
            pivots[i] = jnp.zeros((ROWS, shapes[i][1]), F32)
        for c in range(ROWS):
            for i in live:
                pivot = lines[i][c][c : c + 1]
                factor = jnp.where(at[i] > c, lines[i][c] * (1.0 / pivot), 0.0)
                for d in range(c + 1, ROWS):
                    lines[i][d] = lines[i][d] - factor * lines[i][d][c : c + 1]
                pivots[i] = jnp.where(at[i][:ROWS] == c, pivot, pivots[i])
                works[i] = works[i] - factor * works[i][c : c + 1]
        for i in live:
            finished[i].append(lax.rsqrt(pivots[i]) * works[i][:ROWS])
            works[i] = works[i][ROWS:]
    return [jnp.concatenate(rows, 0)[:, :size] for rows, size in zip(finished, sizes)]


def position(axis):
    return lax.axis_index(axis).astype(jnp.int32)


def send_outer(odd, rounded_ref, last_ref, send_ref):
    @pl.when(odd == 0)
    def _():
        send_ref[...] = rounded_ref[...]

    @pl.when(odd == 1)
    def _():
        send_ref[...] = product(rounded_ref[...], last_ref[...]).astype(BF16)


def send_inner(odd, rounded_ref, last_ref, send_ref):
    end = rounded_ref.shape[0] - 1

    @pl.when(odd == 1)
    def _():
        send_ref[...] = rounded_ref[end]

    @pl.when(odd == 0)
    def _():
        send_ref[...] = product(rounded_ref[end], last_ref[...]).astype(BF16)


def enter_kernel(
    far_bounds_ref, vectors_ref, couplings_ref,
    outer_ref, rest_ref, outer16_ref, rest16_ref, inner_send_ref, outer_send_ref, last_ref, mids_ref, rows_ref,
    bounds_ref, block_ref, sems,
):
    layers = vectors_ref.shape[1]
    copies = [
        pltpu.make_async_copy(vectors_ref, block_ref, sems.at[0]),
        pltpu.make_async_copy(couplings_ref.at[layers - 1], last_ref, sems.at[1]),
        pltpu.make_async_copy(couplings_ref.at[pl.ds(0, layers - 1)], mids_ref.at[0], sems.at[2]),
        pltpu.make_async_copy(far_bounds_ref, bounds_ref, sems.at[3]),
    ]
    for copy in copies:
        copy.start()
    odd = position("layer") % 2
    copies[0].wait()
    for parity in (0, 1):

        @pl.when(odd == parity)
        def _():
            order = range(layers)[:: -1 if parity else 1]
            outer_ref[...] = block_ref[:, order[0], :]
            for i, l in enumerate(order[1:]):
                rest_ref[i] = block_ref[:, l, :]

    outer16_ref[...] = outer_ref[...].astype(BF16)
    rest16_ref[...] = rest_ref[...].astype(BF16)
    copies[1].wait()
    send_outer(odd, outer16_ref, last_ref, outer_send_ref)
    send_inner(odd, rest16_ref, last_ref, inner_send_ref)
    copies[3].wait()
    width = rows_ref.shape[1]
    low, high = bounds_ref[0, 0].astype(F32), bounds_ref[0, 1].astype(F32)
    half = jnp.full((1, width), (high - low) * (1.0 / 128.0), F32)
    rows_ref[0:1] = jnp.full((1, width), (low + high) * (1.0 / 128.0), F32)
    rows_ref[1:2] = 1.0 / half
    rows_ref[2:3] = 2.0 / half
    copies[2].wait()


def turn(matrix_ref, turned_ref):
    size = matrix_ref.shape[0]
    block = 2 * ROWS_FULL if size % (2 * ROWS_FULL) == 0 else size
    for i in range(0, size, block):
        for j in range(0, size, block):
            turned_ref[pl.ds(i, block), pl.ds(j, block)] = jnp.transpose(
                matrix_ref[pl.ds(j, block), pl.ds(i, block)]
            )


def turn_kernel(last_ref, mids_in_ref, last_t_ref, mids_ref):
    turn(last_ref, last_t_ref)
    for i in range(mids_ref.shape[1]):
        turn(mids_in_ref.at[0, i], mids_ref.at[1, i])


def add_arrived(count, scale, base_ref, arrived_ref, last_t_ref, store):
    at = position("layer")
    odd = at % 2

    @pl.when((odd == 0) & (at > 0))
    def _():
        store(base_ref[...] + arrived_ref[...].astype(F32) * scale)

    @pl.when((odd == 1) & (at < count - 1))
    def _():
        store(base_ref[...] + product(arrived_ref[...], last_t_ref[...]) * scale)

    @pl.when((at == 0) | ((odd == 1) & (at == count - 1)))
    def _():
        store(base_ref[...])


def interior_kernel(
    count, layers, step, ahead, gram, adds, final, rows_ref, outer_a_ref, outer_b_ref, rest16_ref, arrived_ref,
    diag_ref, last_ref, last_t_ref, mids_ref, rest_ref, outer_before_ref, rest_before_ref, *refs,
):
    *refs, sum_ref = refs
    outs = list(refs)
    if adds:
        here_ref, there_ref = outs.pop(0), outs.pop(0)
    base_ref, next_ref = outs.pop(0), outs.pop(0)
    first_step = step % DEG == 0
    centre, scale = rows_ref[0:1], rows_ref[1:2] if first_step else rows_ref[2:3]
    odd = position("layer") % 2
    if step:
        outer_ref = outs.pop(0)

        def store(block):
            outer_ref[...] = block

        before = rows_ref[1:2] if (step - 1) % DEG == 0 else rows_ref[2:3]
        add_arrived(count, before, outer_a_ref, outer_b_ref, last_t_ref, store)
        outer16 = outer_ref[...].astype(BF16)
    else:
        outer_ref, outer16 = outer_a_ref, outer_b_ref[...]

    def rounded(place):
        return rest16_ref[place - 1] if place else outer16

    for place in range(layers)[::-1]:
        term = product(rounded(place), diag_ref[place + odd * (layers - 1 - 2 * place)])
        if place < layers - 1:
            link = place + odd * (layers - 2 - 2 * place)
            term = term + product(rounded(place + 1), mids_ref[1 - odd, link])
        if place > 0:
            link = place - 1 + odd * (layers - 2 * place)
            term = term + product(rounded(place - 1), mids_ref[odd, link])
        if place == layers - 1:
            sum_ref[...] = term

            @pl.when(odd == 0)
            def _():
                sum_ref[...] += product(arrived_ref[...], last_t_ref[...])

            @pl.when(odd == 1)
            def _():
                sum_ref[...] += arrived_ref[...].astype(F32)

            term = sum_ref[...]
        if place:
            term = (term - centre * rest_ref[place - 1]) * scale
            next_ref[place - 1] = term if first_step else term - rest_before_ref[place - 1]
        else:
            term = (term - centre * outer_ref[...]) * scale
            base_ref[...] = term if first_step else term - outer_before_ref[...]
    if not final:
        next16_ref, send_ref = outs.pop(0), outs.pop(0)
        next16_ref[...] = next_ref[...].astype(BF16)
        send_inner(odd, next16_ref, last_ref, send_ref)
    if ahead:
        ahead_ref = outs.pop(0)

        @pl.when(odd == 1)
        def _():
            ahead_ref[...] = product(base_ref[...].astype(BF16), last_ref[...])

    if gram:
        outs.pop(0)[...] = product_t(outer_ref[...], outer_ref[...], HIGHEST) + sum(
            product_t(rest_ref[i], rest_ref[i], HIGHEST) for i in range(layers - 1)
        )
    if adds:
        outs.pop(0)[...] = here_ref[...] + there_ref[...]


def square_kernel(part, last_ref, last_t_ref, square_ref):
    size = square_ref.shape[0]

    @pl.when(position("layer") % 2 == 1)
    def _():
        def chunk(i, carry):
            place = pl.multiple_of(i * 2 * ROWS_FULL, 2 * ROWS_FULL)
            rows = last_t_ref[pl.ds(part * size + place, 2 * ROWS_FULL)]
            square_ref[pl.ds(place, 2 * ROWS_FULL)] = product(rows, last_ref[...]).astype(BF16)
            return carry

        lax.fori_loop(0, size // (2 * ROWS_FULL), chunk, 0)


def plain_step_kernel(first_step, rows_ref, base_ref, arrived_ref, last_ref, last_t_ref, *refs):
    send_ref = refs[-1]
    scale = rows_ref[1:2] if first_step else rows_ref[2:3]
    odd = position("layer") % 2

    @pl.when(odd == 0)
    def _():
        has_before = (position("layer") > 0).astype(F32)
        term = arrived_ref[...].astype(F32) * (scale * has_before)
        send_ref[...] = (base_ref[...] + term).astype(BF16)

    @pl.when(odd == 1)
    def _():
        block = base_ref[...] + product(arrived_ref[...], last_t_ref[...]) * scale
        send_ref[...] = product(block.astype(BF16), last_ref[...]).astype(BF16)


def step_kernel(first_step, rows_ref, base_ref, arrived_ref, ahead_ref, square_a_ref, square_b_ref, send_ref):
    scale = rows_ref[1:2] if first_step else rows_ref[2:3]
    odd = position("layer") % 2

    @pl.when(odd == 0)
    def _():
        has_before = (position("layer") > 0).astype(F32)
        term = arrived_ref[...].astype(F32) * (scale * has_before)
        send_ref[...] = (base_ref[...] + term).astype(BF16)

    @pl.when(odd == 1)
    def _():
        half = square_a_ref.shape[0]
        term = product(arrived_ref[:, :half], square_a_ref[...])
        term = term + product(arrived_ref[:, half:], square_b_ref[...])
        block = ahead_ref[...] + term * scale
        send_ref[...] = block.astype(BF16)


def row_scales(gram):
    return lax.rsqrt(jnp.sum(gram * identity(gram.shape[0]), axis=1, keepdims=True))


def scale_kernel(parts, length, *refs):
    grams, (rest_ref, next_ref, next16_ref, gram_ref, scales_ref) = refs[:parts], refs[parts:]
    scales = row_scales(sum(ref[...] for ref in grams) * (1.0 / length))
    scales_ref[...] = jnp.broadcast_to(scales, scales_ref.shape)
    gram_ref[...] = jnp.zeros(gram_ref.shape, F32)
    for i in range(rest_ref.shape[0]):
        block = rest_ref[i] * scales
        next_ref[i] = block
        next16_ref[i] = block.astype(BF16)
        gram_ref[...] += product_t(block, block, HIGHEST)


def last_kernel(
    count, rows_ref, base_ref, arrived_ref, last_t_ref, scales_ref, rest16_ref, rest_gram_ref,
    next_ref, next16_ref, low_ref, gram_ref,
):
    def store(block):
        next_ref[...] = block * scales_ref[:, :1]

    add_arrived(count, rows_ref[2:3], base_ref, arrived_ref, last_t_ref, store)
    next16_ref[...] = next_ref[...].astype(BF16)
    edge = low_ref.shape[1]
    low_ref[0] = next16_ref[:edge]
    for i in range(low_ref.shape[0] - 1):
        low_ref[i + 1] = rest16_ref[i, :edge]
    gram_ref[...] = rest_gram_ref[...] + product_t(next_ref[...], next_ref[...], HIGHEST)


def first_factor_kernel(parts, length, *refs):
    grams, (outer_ref, rest_ref, inverse_ref, all_ref) = refs[:parts], refs[parts:]
    gram = sum(ref[...] for ref in grams) * (1.0 / length)
    scales = row_scales(gram)
    across = jnp.sum(identity(gram.shape[0]) * scales, axis=0, keepdims=True)
    inverse_ref[...] = inverse_factors(gram * scales * across)[0]
    all_ref[0] = exact(inverse_ref[...], outer_ref[...])
    for i in range(rest_ref.shape[0]):
        all_ref[i + 1] = exact(inverse_ref[...], rest_ref[i])


def cross_kernel(gram_ref, outer16_ref, rest16_ref, above_ref, out_ref):
    size, edge = outer16_ref.shape[0], above_ref.shape[1]
    rest = range(rest16_ref.shape[0])
    out_ref[:, :size] = gram_ref[...]
    out_ref[:, size : size + edge] = product_t(outer16_ref[...], above_ref[0]) + sum(
        product_t(rest16_ref[i], above_ref[i + 1]) for i in rest
    )
    out_ref[:edge, size + edge :] = sum(
        product_t(above_ref[l], above_ref[l]) for l in range(above_ref.shape[0])
    )
    out_ref[edge:, size + edge :] = jnp.zeros((size - edge, edge), F32)


def factor_kernel(parts, length, slices, *refs):
    grams, (first_ref, all_ref, inverse_ref, weights_ref, up_ref) = refs[:parts], refs[parts:]
    size, edge = all_ref.shape[1], up_ref.shape[1]
    first = first_ref[...]
    total = sum(ref[...] for ref in grams) * (1.0 / length)
    has_above = (position("cuts") < slices - 1).astype(F32)
    above = total[:edge, size + edge :] * has_above + identity(edge) * (1.0 - has_above)
    cross = exact(first, total[:, size : size + edge]) * has_above
    own = product_t(exact(first, total[:, :size]), first, HIGHEST)
    inverse, above = inverse_factors(own, above)
    inverse_ref[...] = inverse
    high = inverse[size - edge :]
    correlation = product_t(exact(high, cross), above, HIGHEST)
    up = exact(correlation.T, high)
    for i in range(all_ref.shape[0]):
        up_ref[i] = exact(up, all_ref[i]).astype(BF16)
    weights_ref[...] = exact(correlation, above)


def vectors_kernel(inverse_ref, weights_ref, first_ref, above_ref, all_ref):
    layers, size, _ = all_ref.shape
    edge = above_ref.shape[1]
    for i in range(layers):
        block = exact(inverse_ref[...], first_ref[i])
        all_ref[i] = block
        all_ref[i, size - edge :] = block[size - edge :] - exact(
            weights_ref[...], above_ref[i].astype(F32)
        )


def final_kernel(all_ref, below_ref, out_ref):
    layers, size, _ = all_ref.shape
    edge = below_ref.shape[1]
    has_below = (position("cuts") > 0).astype(F32)
    for parity in (0, 1):

        @pl.when(position("layer") % 2 == parity)
        def _():
            for i, l in enumerate(range(layers)[:: -1 if parity else 1]):
                out_ref[:edge, l, :] = all_ref[i, :edge] - below_ref[i].astype(F32) * has_below
                out_ref[edge:, l, :] = all_ref[i, edge:]


def per_device(vectors, diag_blocks, couplings, bounds):
    vectors = vectors[0]
    count_vec, layers, width = vectors.shape
    count, slices = lax.axis_size("layer"), lax.axis_size("cuts")
    length_all = count * layers * width

    def array(dtype, *shape):
        return jax.ShapeDtypeStruct(shape, dtype)

    outer32, outer16 = array(F32, count_vec, width), array(BF16, count_vec, width)
    rest32, rest16 = array(F32, layers - 1, count_vec, width), array(BF16, layers - 1, count_vec, width)
    square = array(F32, count_vec, count_vec)
    matrix = array(BF16, width, width)
    matrices = array(BF16, 2, layers - 1, width, width)
    edges = array(BF16, layers, EDGE, width)
    one = 2 * count_vec * width * width

    def call(kernel, outs, *operands, far=(), scratch_shapes=(), flops=one, aliases=()):
        moved = sum(x.size * x.dtype.itemsize for x in operands)
        return pl.pallas_call(
            kernel,
            out_shape=outs,
            in_specs=[HBM if i in far else VMEM for i in range(len(operands))],
            out_specs=jax.tree.map(lambda _: VMEM, outs),
            scratch_shapes=list(scratch_shapes),
            input_output_aliases=dict(aliases),
            compiler_params=pltpu.CompilerParams(vmem_limit_bytes=32 * 2**20),
            cost_estimate=pl.CostEstimate(flops=flops, bytes_accessed=moved, transcendentals=0),
        )(*operands)

    outer, rest, outer_r, rest_r, inner_send, outer_send, last, mids, rows = call(
        enter_kernel,
        (outer32, rest32, outer16, rest16, outer16, outer16, matrix, matrices, array(F32, 8, width)),
        *map(far_away, (bounds, vectors, couplings)), far=(0, 1, 2),
        scratch_shapes=[
            pltpu.SMEM(bounds.shape, jnp.int32),
            pltpu.VMEM(vectors.shape, F32),
            pltpu.SemaphoreType.DMA((4,)),
        ],
    )

    last_t, mids = call(turn_kernel, (matrix, matrices), last, mids, aliases={1: 1})
    half = array(BF16, width // 2, width)
    squares = [call(functools.partial(square_kernel, i), half, last, last_t) for i in range(2)]
    outer_a, outer_b = outer, outer_r
    outer_now, rest_before = outer, rest
    reaches = doublings()
    applications = STEPS * DEG
    for step in range(applications):
        final, gram = step == applications - 1, step == DEG
        ahead = 1 < step < applications - 1
        adds = step > DEG and bool(reaches) and not final
        outer_in = exchanged(outer_send, 1)
        inner_in = exchanged(inner_send, 0)
        base, rest_next, *extra = call(
            functools.partial(interior_kernel, count, layers, step, ahead, gram, adds, final),
            (outer32, rest32)
            + ((outer32,) if step else ())
            + (() if final else (rest16, outer16))
            + ((outer32,) if ahead else ())
            + ((square,) if gram or adds else ()),
            rows, outer_a, outer_b, rest_r, inner_in, diag_blocks, last, last_t, mids,
            rest, outer_now, rest_before,
            *((total, swapped(total, reaches.pop(0))) if adds else ()),
            scratch_shapes=[pltpu.VMEM((count_vec, width), F32)],
            flops=(3 * layers - 1) * one,
        )
        if step:
            outer_now = extra.pop(0)
        if gram or adds:
            total = extra[-1]
        if gram and not reaches:
            total = lax.psum(total, "layer")
        if final:
            break
        rest_r, inner_send = extra[:2]
        if ahead:
            outer_send = call(
                functools.partial(step_kernel, step % DEG == 0),
                outer16, rows, base, outer_in, extra[2], *squares,
            )
        else:
            outer_send = call(
                functools.partial(plain_step_kernel, step % DEG == 0),
                outer16, rows, base, outer_in, last, last_t, *squares[:step],
            )
        outer_a, outer_b = base, outer_in
        rest_before, rest = rest, rest_next

    totals = [total]
    for reach in reaches:
        totals = [sum(totals), swapped(sum(totals), reach)]
    rest, rest_r, rest_gram, scales = call(
        functools.partial(scale_kernel, len(totals), length_all),
        (rest32, rest16, square, array(F32, count_vec, 128)), *totals, rest_next,
    )
    outer, outer_r, low, gram = call(
        functools.partial(last_kernel, count), (outer32, outer16, edges, square),
        rows, base, outer_in, last_t, scales, rest_r, rest_gram,
    )
    above = rotated(low, -1)
    field32 = array(F32, layers, count_vec, width)
    cross = call(
        cross_kernel, array(F32, count_vec, count_vec + 2 * EDGE), gram, outer_r, rest_r, above
    )
    first, first_all = call(
        functools.partial(first_factor_kernel, len(totals), length_all),
        (square, field32), *totals, outer, rest,
    )
    grams = partial_sums(cross)
    inverse, weights, up = call(
        functools.partial(factor_kernel, len(grams), length_all, slices),
        (square, array(F32, EDGE, EDGE), edges), *grams, first, first_all,
    )
    below = rotated(up, 1)
    vectors_all = call(vectors_kernel, field32, inverse, weights, first_all, above)
    result = call(final_kernel, array(F32, count_vec, layers, width), vectors_all, below)
    return result[None]


def solution(mesh):
    in_specs = (
        P("cuts", None, "layer", None),
        P("layer", None, None),
        P("layer", None, None),
        P("cuts", None),
    )
    out_specs = P("cuts", None, "layer", None)
    return jax.shard_map(
        per_device, mesh=mesh, in_specs=in_specs, out_specs=out_specs, check_vma=False
    )
```

```python
import functools

import jax
import jax.numpy as jnp
from jax import lax
from jax.experimental import pallas as pl
from jax.experimental.pallas import tpu as pltpu
from jax.sharding import PartitionSpec as P

EDGE = 16
DEG = 4
STEPS = 2
ROWS = 16
ROWS_FULL = 128
HIGHEST = lax.Precision.HIGHEST
BF16 = jnp.bfloat16
F32 = jnp.float32
VMEM = pl.BlockSpec(memory_space=pltpu.VMEM)
HBM = pl.BlockSpec(memory_space=pltpu.HBM)


def exchanged(block, first):
    count, slices = lax.axis_size("layer"), lax.axis_size("cuts")
    route = []
    for cut in range(slices):
        for i in range(count):
            j = i + 1 if (i - first) % 2 == 0 else i - 1
            to = (cut, j) if 0 <= j < count else (cut ^ 1 if cut ^ 1 < slices else cut, i)
            route.append((cut * count + i, to[0] * count + to[1]))
    return lax.ppermute(block, ("cuts", "layer"), route)


def far_away(block):
    return pltpu.with_memory_space_constraint(block, pltpu.HBM)


def rotated(block, distance):
    size = lax.axis_size("cuts")
    return lax.ppermute(block, "cuts", [(i, (i + distance) % size) for i in range(size)])


def doublings():
    size = lax.axis_size("layer")
    return [] if size & (size - 1) else [1 << i for i in range(size.bit_length() - 1)]


def swapped(block, reach):
    far = reach | 1
    return lax.ppermute(block, "layer", [(i, i ^ far) for i in range(lax.axis_size("layer"))])


def partial_sums(block):
    size = lax.axis_size("layer")
    if not doublings():
        return [lax.psum(block, "layer")]
    reach = 1
    while size // reach > 4:
        block = block + swapped(block, reach)
        reach *= 2
    return [block] + [swapped(block, step) for step in range(reach, size, reach)]


def product(block, matrix):
    size = block.shape[0]
    block = jnp.concatenate([block] * max(1, ROWS_FULL // size), 0)
    return jnp.dot(block, matrix, preferred_element_type=F32)[:size]


def product_t(block, matrix, precision=None):
    return lax.dot_general(
        block, matrix, (((1,), (1,)), ((), ())), precision=precision, preferred_element_type=F32
    )


def exact(first, second):
    return jnp.dot(first, second, precision=HIGHEST, preferred_element_type=F32)


def identity(size):
    row = lax.broadcasted_iota(jnp.int32, (size, size), 0)
    column = lax.broadcasted_iota(jnp.int32, (size, size), 1)
    return jnp.where(row == column, 1.0, 0.0)


def inverse_factors(*grams):
    sizes = [gram.shape[0] for gram in grams]
    works = [jnp.concatenate([identity(gram.shape[0]), gram], 1) for gram in grams]
    finished = [[] for _ in grams]
    for start in range(0, max(sizes), ROWS):
        live = [i for i, size in enumerate(sizes) if start < size]
        shapes = {i: (sizes[i] - start, 2 * sizes[i]) for i in live}
        at = {i: lax.broadcasted_iota(jnp.int32, shapes[i], 0) for i in live}
        lines, pivots = {}, {}
        for i in live:
            first = sizes[i] + start
            lines[i] = [
                jnp.broadcast_to(works[i][:, first + c : first + c + 1], shapes[i])
                for c in range(ROWS)
            ]
            pivots[i] = jnp.zeros((ROWS, shapes[i][1]), F32)
        for c in range(ROWS):
            for i in live:
                pivot = lines[i][c][c : c + 1]
                factor = jnp.where(at[i] > c, lines[i][c] * (1.0 / pivot), 0.0)
                for d in range(c + 1, ROWS):
                    lines[i][d] = lines[i][d] - factor * lines[i][d][c : c + 1]
                pivots[i] = jnp.where(at[i][:ROWS] == c, pivot, pivots[i])
                works[i] = works[i] - factor * works[i][c : c + 1]
        for i in live:
            finished[i].append(lax.rsqrt(pivots[i]) * works[i][:ROWS])
            works[i] = works[i][ROWS:]
    return [jnp.concatenate(rows, 0)[:, :size] for rows, size in zip(finished, sizes)]


def position(axis):
    return lax.axis_index(axis).astype(jnp.int32)


def send_outer(odd, rounded_ref, last_ref, send_ref):
    @pl.when(odd == 0)
    def _():
        send_ref[...] = rounded_ref[...]

    @pl.when(odd == 1)
    def _():
        send_ref[...] = product(rounded_ref[...], last_ref[...]).astype(BF16)


def send_inner(odd, rounded_ref, last_ref, send_ref):
    end = rounded_ref.shape[0] - 1

    @pl.when(odd == 1)
    def _():
        send_ref[...] = rounded_ref[end]

    @pl.when(odd == 0)
    def _():
        send_ref[...] = product(rounded_ref[end], last_ref[...]).astype(BF16)


def enter_kernel(
    far_bounds_ref, vectors_ref, couplings_ref,
    outer_ref, rest_ref, outer16_ref, rest16_ref, inner_send_ref, outer_send_ref, last_ref, mids_ref, rows_ref,
    bounds_ref, block_ref, sems,
):
    layers = vectors_ref.shape[1]
    copies = [
        pltpu.make_async_copy(vectors_ref, block_ref, sems.at[0]),
        pltpu.make_async_copy(couplings_ref.at[layers - 1], last_ref, sems.at[1]),
        pltpu.make_async_copy(couplings_ref.at[pl.ds(0, layers - 1)], mids_ref.at[0], sems.at[2]),
        pltpu.make_async_copy(far_bounds_ref, bounds_ref, sems.at[3]),
    ]
    for copy in copies:
        copy.start()
    odd = position("layer") % 2
    copies[0].wait()
    for parity in (0, 1):

        @pl.when(odd == parity)
        def _():
            order = range(layers)[:: -1 if parity else 1]
            outer_ref[...] = block_ref[:, order[0], :]
            for i, l in enumerate(order[1:]):
                rest_ref[i] = block_ref[:, l, :]

    outer16_ref[...] = outer_ref[...].astype(BF16)
    rest16_ref[...] = rest_ref[...].astype(BF16)
    copies[1].wait()
    send_outer(odd, outer16_ref, last_ref, outer_send_ref)
    send_inner(odd, rest16_ref, last_ref, inner_send_ref)
    copies[3].wait()
    width = rows_ref.shape[1]
    low, high = bounds_ref[0, 0].astype(F32), bounds_ref[0, 1].astype(F32)
    half = jnp.full((1, width), (high - low) * (1.0 / 128.0), F32)
    rows_ref[0:1] = jnp.full((1, width), (low + high) * (1.0 / 128.0), F32)
    rows_ref[1:2] = 1.0 / half
    rows_ref[2:3] = 2.0 / half
    copies[2].wait()


def turn(matrix_ref, turned_ref):
    size = matrix_ref.shape[0]
    block = 2 * ROWS_FULL if size % (2 * ROWS_FULL) == 0 else size
    for i in range(0, size, block):
        for j in range(0, size, block):
            turned_ref[pl.ds(i, block), pl.ds(j, block)] = jnp.transpose(
                matrix_ref[pl.ds(j, block), pl.ds(i, block)]
            )


def turn_kernel(last_ref, mids_in_ref, last_t_ref, mids_ref):
    turn(last_ref, last_t_ref)
    for i in range(mids_ref.shape[1]):
        turn(mids_in_ref.at[0, i], mids_ref.at[1, i])


def add_arrived(count, scale, base_ref, arrived_ref, last_t_ref, store):
    at = position("layer")
    odd = at % 2

    @pl.when((odd == 0) & (at > 0))
    def _():
        store(base_ref[...] + arrived_ref[...].astype(F32) * scale)

    @pl.when((odd == 1) & (at < count - 1))
    def _():
        store(base_ref[...] + product(arrived_ref[...], last_t_ref[...]) * scale)

    @pl.when((at == 0) | ((odd == 1) & (at == count - 1)))
    def _():
        store(base_ref[...])


def interior_kernel(
    count, layers, step, ahead, gram, adds, final, rows_ref, outer_a_ref, outer_b_ref, rest16_ref, arrived_ref,
    diag_ref, last_ref, last_t_ref, mids_ref, rest_ref, outer_before_ref, rest_before_ref, *refs,
):
    *refs, sum_ref = refs
    outs = list(refs)
    if adds:
        here_ref, there_ref = outs.pop(0), outs.pop(0)
    base_ref, next_ref = outs.pop(0), outs.pop(0)
    first_step = step % DEG == 0
    centre, scale = rows_ref[0:1], rows_ref[1:2] if first_step else rows_ref[2:3]
    odd = position("layer") % 2
    if step:
        outer_ref = outs.pop(0)

        def store(block):
            outer_ref[...] = block

        before = rows_ref[1:2] if (step - 1) % DEG == 0 else rows_ref[2:3]
        add_arrived(count, before, outer_a_ref, outer_b_ref, last_t_ref, store)
        outer16 = outer_ref[...].astype(BF16)
    else:
        outer_ref, outer16 = outer_a_ref, outer_b_ref[...]

    def rounded(place):
        return rest16_ref[place - 1] if place else outer16

    for place in range(layers)[::-1]:
        term = product(rounded(place), diag_ref[place + odd * (layers - 1 - 2 * place)])
        if place < layers - 1:
            link = place + odd * (layers - 2 - 2 * place)
            term = term + product(rounded(place + 1), mids_ref[1 - odd, link])
        if place > 0:
            link = place - 1 + odd * (layers - 2 * place)
            term = term + product(rounded(place - 1), mids_ref[odd, link])
        if place == layers - 1:
            sum_ref[...] = term

            @pl.when(odd == 0)
            def _():
                sum_ref[...] += product(arrived_ref[...], last_t_ref[...])

            @pl.when(odd == 1)
            def _():
                sum_ref[...] += arrived_ref[...].astype(F32)

            term = sum_ref[...]
        if place:
            term = (term - centre * rest_ref[place - 1]) * scale
            next_ref[place - 1] = term if first_step else term - rest_before_ref[place - 1]
        else:
            term = (term - centre * outer_ref[...]) * scale
            base_ref[...] = term if first_step else term - outer_before_ref[...]
    if not final:
        next16_ref, send_ref = outs.pop(0), outs.pop(0)
        next16_ref[...] = next_ref[...].astype(BF16)
        send_inner(odd, next16_ref, last_ref, send_ref)
    if ahead:
        ahead_ref = outs.pop(0)

        @pl.when(odd == 1)
        def _():
            ahead_ref[...] = product(base_ref[...].astype(BF16), last_ref[...])

    if gram:
        outs.pop(0)[...] = product_t(outer_ref[...], outer_ref[...], HIGHEST) + sum(
            product_t(rest_ref[i], rest_ref[i], HIGHEST) for i in range(layers - 1)
        )
    if adds:
        outs.pop(0)[...] = here_ref[...] + there_ref[...]


def square_kernel(part, last_ref, last_t_ref, square_ref):
    size = square_ref.shape[0]

    @pl.when(position("layer") % 2 == 1)
    def _():
        def chunk(i, carry):
            place = pl.multiple_of(i * 2 * ROWS_FULL, 2 * ROWS_FULL)
            rows = last_t_ref[pl.ds(part * size + place, 2 * ROWS_FULL)]
            square_ref[pl.ds(place, 2 * ROWS_FULL)] = product(rows, last_ref[...]).astype(BF16)
            return carry

        lax.fori_loop(0, size // (2 * ROWS_FULL), chunk, 0)


def plain_step_kernel(first_step, rows_ref, base_ref, arrived_ref, last_ref, last_t_ref, *refs):
    send_ref = refs[-1]
    scale = rows_ref[1:2] if first_step else rows_ref[2:3]
    odd = position("layer") % 2

    @pl.when(odd == 0)
    def _():
        has_before = (position("layer") > 0).astype(F32)
        term = arrived_ref[...].astype(F32) * (scale * has_before)
        send_ref[...] = (base_ref[...] + term).astype(BF16)

    @pl.when(odd == 1)
    def _():
        block = base_ref[...] + product(arrived_ref[...], last_t_ref[...]) * scale
        send_ref[...] = product(block.astype(BF16), last_ref[...]).astype(BF16)


def step_kernel(first_step, rows_ref, base_ref, arrived_ref, ahead_ref, square_a_ref, square_b_ref, send_ref):
    scale = rows_ref[1:2] if first_step else rows_ref[2:3]
    odd = position("layer") % 2

    @pl.when(odd == 0)
    def _():
        has_before = (position("layer") > 0).astype(F32)
        term = arrived_ref[...].astype(F32) * (scale * has_before)
        send_ref[...] = (base_ref[...] + term).astype(BF16)

    @pl.when(odd == 1)
    def _():
        half = square_a_ref.shape[0]
        term = product(arrived_ref[:, :half], square_a_ref[...])
        term = term + product(arrived_ref[:, half:], square_b_ref[...])
        block = ahead_ref[...] + term * scale
        send_ref[...] = block.astype(BF16)


def row_scales(gram):
    return lax.rsqrt(jnp.sum(gram * identity(gram.shape[0]), axis=1, keepdims=True))


def outer_kernel(count, rows_ref, base_ref, arrived_ref, last_t_ref, next_ref):
    def store(block):
        next_ref[...] = block

    add_arrived(count, rows_ref[2:3], base_ref, arrived_ref, last_t_ref, store)


def scale_kernel(parts, length, *refs):
    grams, (outer_ref, rest_ref, all_ref, all16_ref, low_ref, gram_ref) = refs[:parts], refs[parts:]
    scales = row_scales(sum(ref[...] for ref in grams) * (1.0 / length))
    edge = low_ref.shape[1]
    total = 0.0
    for i in range(all_ref.shape[0]):
        block = (rest_ref[i - 1] if i else outer_ref[...]) * scales
        all_ref[i] = block
        rounded = block.astype(BF16)
        all16_ref[i] = rounded
        low_ref[i] = rounded[:edge]
        total = total + product_t(block, block, HIGHEST)
    gram_ref[...] = total


def first_factor_kernel(parts, length, *refs):
    grams, (scaled_ref, inverse_ref, all_ref) = refs[:parts], refs[parts:]
    gram = sum(ref[...] for ref in grams) * (1.0 / length)
    scales = row_scales(gram)
    across = jnp.sum(identity(gram.shape[0]) * scales, axis=0, keepdims=True)
    inverse_ref[...] = inverse_factors(gram * scales * across)[0]
    for i in range(all_ref.shape[0]):
        all_ref[i] = exact(inverse_ref[...], scaled_ref[i])


def cross_kernel(gram_ref, all16_ref, above_ref, out_ref):
    size, edge = gram_ref.shape[0], above_ref.shape[1]
    places = range(above_ref.shape[0])
    out_ref[:, :size] = gram_ref[...]
    out_ref[:, size : size + edge] = sum(product_t(all16_ref[i], above_ref[i]) for i in places)
    out_ref[:edge, size + edge :] = sum(product_t(above_ref[i], above_ref[i]) for i in places)
    out_ref[edge:, size + edge :] = jnp.zeros((size - edge, edge), F32)


def factor_kernel(parts, length, slices, *refs):
    grams, (first_ref, all_ref, inverse_ref, weights_ref, up_ref) = refs[:parts], refs[parts:]
    size, edge = all_ref.shape[1], up_ref.shape[1]
    first = first_ref[...]
    total = sum(ref[...] for ref in grams) * (1.0 / length)
    has_above = (position("cuts") < slices - 1).astype(F32)
    above = total[:edge, size + edge :] * has_above + identity(edge) * (1.0 - has_above)
    cross = exact(first, total[:, size : size + edge]) * has_above
    own = product_t(exact(first, total[:, :size]), first, HIGHEST)
    inverse, above = inverse_factors(own, above)
    inverse_ref[...] = inverse
    high = inverse[size - edge :]
    correlation = product_t(exact(high, cross), above, HIGHEST)
    up = exact(correlation.T, high)
    for i in range(all_ref.shape[0]):
        up_ref[i] = jnp.dot(up.astype(BF16), all_ref[i].astype(BF16), preferred_element_type=F32).astype(BF16)
    weights_ref[...] = exact(correlation, above)


def by_layer(layers, store):
    for parity in (0, 1):

        @pl.when(position("layer") % 2 == parity)
        def _():
            for place, layer in enumerate(range(layers)[:: -1 if parity else 1]):
                store(layer, place)


def vectors_kernel(inverse_ref, weights_ref, first_ref, above_ref, low_ref, out_ref, block_ref, sem):
    layers, size, _ = first_ref.shape
    edge = low_ref.shape[1]
    blocks = []
    for i in range(layers):
        block = exact(inverse_ref[...], first_ref[i])
        high = block[size - edge :] - exact(weights_ref[...], above_ref[i].astype(F32))
        low_ref[i] = block[:edge]
        blocks.append(jnp.concatenate([block[edge : size - edge], high], 0))

    def store(layer, place):
        block_ref[:, layer, :] = blocks[place]

    by_layer(layers, store)
    copy = pltpu.make_async_copy(block_ref, out_ref.at[pl.ds(edge, size - edge)], sem)
    copy.start()
    copy.wait()


def final_kernel(low_ref, below_ref, _, out_ref, block_ref, sem):
    layers, edge, _ = low_ref.shape
    has_below = (position("cuts") > 0).astype(F32)

    def store(layer, place):
        block_ref[:, layer, :] = low_ref[place] - below_ref[place].astype(F32) * has_below

    by_layer(layers, store)
    copy = pltpu.make_async_copy(block_ref, out_ref.at[pl.ds(0, edge)], sem)
    copy.start()
    copy.wait()


def per_device(vectors, diag_blocks, couplings, bounds):
    vectors = vectors[0]
    count_vec, layers, width = vectors.shape
    count, slices = lax.axis_size("layer"), lax.axis_size("cuts")
    length_all = count * layers * width

    def array(dtype, *shape):
        return jax.ShapeDtypeStruct(shape, dtype)

    outer32, outer16 = array(F32, count_vec, width), array(BF16, count_vec, width)
    rest32, rest16 = array(F32, layers - 1, count_vec, width), array(BF16, layers - 1, count_vec, width)
    square = array(F32, count_vec, count_vec)
    matrix = array(BF16, width, width)
    matrices = array(BF16, 2, layers - 1, width, width)
    edges = array(BF16, layers, EDGE, width)
    one = 2 * count_vec * width * width

    def call(kernel, outs, *operands, far=(), far_out=(), scratch_shapes=(), flops=one, aliases=()):
        moved = sum(x.size * x.dtype.itemsize for x in operands)
        return pl.pallas_call(
            kernel,
            out_shape=outs,
            in_specs=[HBM if i in far else VMEM for i in range(len(operands))],
            out_specs=(
                tuple(HBM if i in far_out else VMEM for i in range(len(outs)))
                if isinstance(outs, tuple)
                else VMEM
            ),
            scratch_shapes=list(scratch_shapes),
            input_output_aliases=dict(aliases),
            compiler_params=pltpu.CompilerParams(vmem_limit_bytes=32 * 2**20),
            cost_estimate=pl.CostEstimate(flops=flops, bytes_accessed=moved, transcendentals=0),
        )(*operands)

    outer, rest, outer_r, rest_r, inner_send, outer_send, last, mids, rows = call(
        enter_kernel,
        (outer32, rest32, outer16, rest16, outer16, outer16, matrix, matrices, array(F32, 8, width)),
        *map(far_away, (bounds, vectors, couplings)), far=(0, 1, 2),
        scratch_shapes=[
            pltpu.SMEM(bounds.shape, jnp.int32),
            pltpu.VMEM(vectors.shape, F32),
            pltpu.SemaphoreType.DMA((4,)),
        ],
    )

    last_t, mids = call(turn_kernel, (matrix, matrices), last, mids, aliases={1: 1})
    half = array(BF16, width // 2, width)
    squares = [call(functools.partial(square_kernel, i), half, last, last_t) for i in range(2)]
    outer_a, outer_b = outer, outer_r
    outer_now, rest_before = outer, rest
    reaches = doublings()
    applications = STEPS * DEG
    for step in range(applications):
        final, gram = step == applications - 1, step == DEG
        ahead = 1 < step < applications - 1
        adds = step > DEG and bool(reaches) and not final
        outer_in = exchanged(outer_send, 1)
        inner_in = exchanged(inner_send, 0)
        base, rest_next, *extra = call(
            functools.partial(interior_kernel, count, layers, step, ahead, gram, adds, final),
            (outer32, rest32)
            + ((outer32,) if step else ())
            + (() if final else (rest16, outer16))
            + ((outer32,) if ahead else ())
            + ((square,) if gram or adds else ()),
            rows, outer_a, outer_b, rest_r, inner_in, diag_blocks, last, last_t, mids,
            rest, outer_now, rest_before,
            *((total, swapped(total, reaches.pop(0))) if adds else ()),
            scratch_shapes=[pltpu.VMEM((count_vec, width), F32)],
            flops=int(2 * (3 * layers - 1) * one),
        )
        if step:
            outer_now = extra.pop(0)
        if gram or adds:
            total = extra[-1]
        if gram and not reaches:
            total = lax.psum(total, "layer")
        if final:
            break
        rest_r, inner_send = extra[:2]
        if ahead:
            outer_send = call(
                functools.partial(step_kernel, step % DEG == 0),
                outer16, rows, base, outer_in, extra[2], *squares,
            )
        else:
            outer_send = call(
                functools.partial(plain_step_kernel, step % DEG == 0),
                outer16, rows, base, outer_in, last, last_t, *squares[:step],
            )
        outer_a, outer_b = base, outer_in
        rest_before, rest = rest, rest_next

    totals = [total]
    for reach in reaches:
        totals = [sum(totals), swapped(sum(totals), reach)]
    outer = call(functools.partial(outer_kernel, count), outer32, rows, base, outer_in, last_t)
    field32 = array(F32, layers, count_vec, width)
    field16 = array(BF16, layers, count_vec, width)
    scaled, scaled_r, low, gram = call(
        functools.partial(scale_kernel, len(totals), length_all),
        (field32, field16, edges, square), *totals, outer, rest_next,
    )
    above = rotated(low, -1)
    cross = call(
        cross_kernel, array(F32, count_vec, count_vec + 2 * EDGE), gram, scaled_r, above
    )
    first, first_all = call(
        functools.partial(first_factor_kernel, len(totals), length_all),
        (square, field32), *totals, scaled,
    )
    grams = partial_sums(cross)
    inverse, weights, up = call(
        functools.partial(factor_kernel, len(grams), length_all, slices),
        (square, array(F32, EDGE, EDGE), edges), *grams, first, first_all,
    )
    below = rotated(up, 1)
    whole = array(F32, count_vec, layers, width)
    low, result = call(
        vectors_kernel, (array(F32, layers, EDGE, width), whole),
        inverse, weights, first_all, above, far_out=(1,),
        scratch_shapes=[
            pltpu.VMEM((count_vec - EDGE, layers, width), F32), pltpu.SemaphoreType.DMA,
        ],
    )
    (result,) = call(
        final_kernel, (whole,), low, below, result, far=(2,), far_out=(0,), aliases={2: 0},
        scratch_shapes=[pltpu.VMEM((EDGE, layers, width), F32), pltpu.SemaphoreType.DMA],
    )
    return result[None]


def solution(mesh):
    in_specs = (
        P("cuts", None, "layer", None),
        P("layer", None, None),
        P("layer", None, None),
        P("cuts", None),
    )
    out_specs = P("cuts", None, "layer", None)
    return jax.shard_map(
        per_device, mesh=mesh, in_specs=in_specs, out_specs=out_specs, check_vma=False
    )
```

```python
import functools

import jax
import jax.numpy as jnp
from jax import lax
from jax.experimental import pallas as pl
from jax.experimental.pallas import tpu as pltpu
from jax.sharding import PartitionSpec as P

EDGE = 16
DEG = 4
STEPS = 2
ROWS = 16
ROWS_FULL = 128
HIGHEST = lax.Precision.HIGHEST
BF16 = jnp.bfloat16
F32 = jnp.float32
VMEM = pl.BlockSpec(memory_space=pltpu.VMEM)
HBM = pl.BlockSpec(memory_space=pltpu.HBM)


def exchanged(block, first):
    count, slices = lax.axis_size("layer"), lax.axis_size("cuts")
    route = []
    for cut in range(slices):
        for i in range(count):
            j = i + 1 if (i - first) % 2 == 0 else i - 1
            to = (cut, j) if 0 <= j < count else (cut ^ 1 if cut ^ 1 < slices else cut, i)
            route.append((cut * count + i, to[0] * count + to[1]))
    return lax.ppermute(block, ("cuts", "layer"), route)


def far_away(block):
    return pltpu.with_memory_space_constraint(block, pltpu.HBM)


def rotated(block, distance):
    size = lax.axis_size("cuts")
    return lax.ppermute(block, "cuts", [(i, (i + distance) % size) for i in range(size)])


def doublings():
    size = lax.axis_size("layer")
    return [] if size & (size - 1) else [1 << i for i in range(size.bit_length() - 1)]


def swapped(block, reach):
    far = reach | 1
    return lax.ppermute(block, "layer", [(i, i ^ far) for i in range(lax.axis_size("layer"))])


def partial_sums(block):
    size = lax.axis_size("layer")
    if not doublings():
        return [lax.psum(block, "layer")]
    reach = 1
    while size // reach > 4:
        block = block + swapped(block, reach)
        reach *= 2
    steps = sorted(range(reach, size, reach), key=lambda step: (step == size - reach, -step))
    return [block] + [swapped(block, step) for step in steps]


def product(block, matrix):
    size = block.shape[0]
    block = jnp.concatenate([block] * max(1, ROWS_FULL // size), 0)
    return jnp.dot(block, matrix, preferred_element_type=F32)[:size]


def product_t(block, matrix, precision=None):
    return lax.dot_general(
        block, matrix, (((1,), (1,)), ((), ())), precision=precision, preferred_element_type=F32
    )


def exact(first, second):
    return jnp.dot(first, second, precision=HIGHEST, preferred_element_type=F32)


def identity(size):
    row = lax.broadcasted_iota(jnp.int32, (size, size), 0)
    column = lax.broadcasted_iota(jnp.int32, (size, size), 1)
    return jnp.where(row == column, 1.0, 0.0)


def inverse_factors(*grams):
    sizes = [gram.shape[0] for gram in grams]
    works = [jnp.concatenate([identity(gram.shape[0]), gram], 1) for gram in grams]
    finished = [[] for _ in grams]
    for start in range(0, max(sizes), ROWS):
        live = [i for i, size in enumerate(sizes) if start < size]
        shapes = {i: (sizes[i] - start, 2 * sizes[i]) for i in live}
        at = {i: lax.broadcasted_iota(jnp.int32, shapes[i], 0) for i in live}
        lines, pivots = {}, {}
        for i in live:
            first = sizes[i] + start
            lines[i] = [
                jnp.broadcast_to(works[i][:, first + c : first + c + 1], shapes[i])
                for c in range(ROWS)
            ]
            pivots[i] = jnp.zeros((ROWS, shapes[i][1]), F32)
        for c in range(ROWS):
            for i in live:
                pivot = lines[i][c][c : c + 1]
                factor = jnp.where(at[i] > c, lines[i][c] * (1.0 / pivot), 0.0)
                for d in range(c + 1, ROWS):
                    lines[i][d] = lines[i][d] - factor * lines[i][d][c : c + 1]
                pivots[i] = jnp.where(at[i][:ROWS] == c, pivot, pivots[i])
                works[i] = works[i] - factor * works[i][c : c + 1]
        for i in live:
            finished[i].append(lax.rsqrt(pivots[i]) * works[i][:ROWS])
            works[i] = works[i][ROWS:]
    return [jnp.concatenate(rows, 0)[:, :size] for rows, size in zip(finished, sizes)]


def position(axis):
    return lax.axis_index(axis).astype(jnp.int32)


def send_outer(odd, rounded_ref, last_ref, send_ref):
    @pl.when(odd == 0)
    def _():
        send_ref[...] = rounded_ref[...]

    @pl.when(odd == 1)
    def _():
        send_ref[...] = product(rounded_ref[...], last_ref[...]).astype(BF16)


def send_inner(odd, rounded_ref, last_ref, send_ref):
    end = rounded_ref.shape[0] - 1

    @pl.when(odd == 1)
    def _():
        send_ref[...] = rounded_ref[end]

    @pl.when(odd == 0)
    def _():
        send_ref[...] = product(rounded_ref[end], last_ref[...]).astype(BF16)


def enter_kernel(
    far_bounds_ref, vectors_ref, couplings_ref,
    outer_ref, rest_ref, outer16_ref, rest16_ref, inner_send_ref, outer_send_ref, last_ref, mids_ref, rows_ref,
    bounds_ref, block_ref, sems,
):
    layers = vectors_ref.shape[1]
    copies = [
        pltpu.make_async_copy(vectors_ref, block_ref, sems.at[0]),
        pltpu.make_async_copy(couplings_ref.at[layers - 1], last_ref, sems.at[1]),
        pltpu.make_async_copy(couplings_ref.at[pl.ds(0, layers - 1)], mids_ref.at[0], sems.at[2]),
        pltpu.make_async_copy(far_bounds_ref, bounds_ref, sems.at[3]),
    ]
    for copy in copies:
        copy.start()
    odd = position("layer") % 2
    copies[0].wait()
    for parity in (0, 1):

        @pl.when(odd == parity)
        def _():
            order = range(layers)[:: -1 if parity else 1]
            outer_ref[...] = block_ref[:, order[0], :]
            for i, l in enumerate(order[1:]):
                rest_ref[i] = block_ref[:, l, :]

    outer16_ref[...] = outer_ref[...].astype(BF16)
    rest16_ref[...] = rest_ref[...].astype(BF16)
    copies[1].wait()
    send_outer(odd, outer16_ref, last_ref, outer_send_ref)
    send_inner(odd, rest16_ref, last_ref, inner_send_ref)
    copies[3].wait()
    width = rows_ref.shape[1]
    low, high = bounds_ref[0, 0].astype(F32), bounds_ref[0, 1].astype(F32)
    half = jnp.full((1, width), (high - low) * (1.0 / 128.0), F32)
    rows_ref[0:1] = jnp.full((1, width), (low + high) * (1.0 / 128.0), F32)
    rows_ref[1:2] = 1.0 / half
    rows_ref[2:3] = 2.0 / half
    copies[2].wait()


def turn(matrix_ref, turned_ref):
    size = matrix_ref.shape[0]
    block = 2 * ROWS_FULL if size % (2 * ROWS_FULL) == 0 else size
    for i in range(0, size, block):
        for j in range(0, size, block):
            turned_ref[pl.ds(i, block), pl.ds(j, block)] = jnp.transpose(
                matrix_ref[pl.ds(j, block), pl.ds(i, block)]
            )


def turn_kernel(last_ref, mids_in_ref, last_t_ref, mids_ref):
    turn(last_ref, last_t_ref)
    for i in range(mids_ref.shape[1]):
        turn(mids_in_ref.at[0, i], mids_ref.at[1, i])


def add_arrived(count, scale, base_ref, arrived_ref, last_t_ref, store):
    at = position("layer")
    odd = at % 2

    @pl.when((odd == 0) & (at > 0))
    def _():
        store(base_ref[...] + arrived_ref[...].astype(F32) * scale)

    @pl.when((odd == 1) & (at < count - 1))
    def _():
        store(base_ref[...] + product(arrived_ref[...], last_t_ref[...]) * scale)

    @pl.when((at == 0) | ((odd == 1) & (at == count - 1)))
    def _():
        store(base_ref[...])


def interior_kernel(
    count, layers, step, ahead, gram, adds, final, rows_ref, outer_a_ref, outer_b_ref, rest16_ref, arrived_ref,
    diag_ref, last_ref, last_t_ref, mids_ref, rest_ref, outer_before_ref, rest_before_ref, *refs,
):
    *refs, sum_ref = refs
    outs = list(refs)
    if adds:
        here_ref, there_ref = outs.pop(0), outs.pop(0)
    base_ref, next_ref = outs.pop(0), outs.pop(0)
    first_step = step % DEG == 0
    centre, scale = rows_ref[0:1], rows_ref[1:2] if first_step else rows_ref[2:3]
    odd = position("layer") % 2
    if step:
        outer_ref = outs.pop(0)

        def store(block):
            outer_ref[...] = block

        before = rows_ref[1:2] if (step - 1) % DEG == 0 else rows_ref[2:3]
        add_arrived(count, before, outer_a_ref, outer_b_ref, last_t_ref, store)
        outer16 = outer_ref[...].astype(BF16)
    else:
        outer_ref, outer16 = outer_a_ref, outer_b_ref[...]

    def rounded(place):
        return rest16_ref[place - 1] if place else outer16

    for place in range(layers)[::-1]:
        term = product(rounded(place), diag_ref[place + odd * (layers - 1 - 2 * place)])
        if place < layers - 1:
            link = place + odd * (layers - 2 - 2 * place)
            term = term + product(rounded(place + 1), mids_ref[1 - odd, link])
        if place > 0:
            link = place - 1 + odd * (layers - 2 * place)
            term = term + product(rounded(place - 1), mids_ref[odd, link])
        if place == layers - 1:
            sum_ref[...] = term

            @pl.when(odd == 0)
            def _():
                sum_ref[...] += product(arrived_ref[...], last_t_ref[...])

            @pl.when(odd == 1)
            def _():
                sum_ref[...] += arrived_ref[...].astype(F32)

            term = sum_ref[...]
        if place:
            term = (term - centre * rest_ref[place - 1]) * scale
            next_ref[place - 1] = term if first_step else term - rest_before_ref[place - 1]
        else:
            term = (term - centre * outer_ref[...]) * scale
            base_ref[...] = term if first_step else term - outer_before_ref[...]
    if not final:
        next16_ref, send_ref = outs.pop(0), outs.pop(0)
        next16_ref[...] = next_ref[...].astype(BF16)
        send_inner(odd, next16_ref, last_ref, send_ref)
    if ahead:
        ahead_ref = outs.pop(0)

        @pl.when(odd == 1)
        def _():
            ahead_ref[...] = product(base_ref[...].astype(BF16), last_ref[...])

    if gram:
        outs.pop(0)[...] = product_t(outer_ref[...], outer_ref[...], HIGHEST) + sum(
            product_t(rest_ref[i], rest_ref[i], HIGHEST) for i in range(layers - 1)
        )
    if adds:
        outs.pop(0)[...] = here_ref[...] + there_ref[...]


def square_kernel(part, last_ref, last_t_ref, square_ref):
    size = square_ref.shape[0]

    @pl.when(position("layer") % 2 == 1)
    def _():
        def chunk(i, carry):
            place = pl.multiple_of(i * 2 * ROWS_FULL, 2 * ROWS_FULL)
            rows = last_t_ref[pl.ds(part * size + place, 2 * ROWS_FULL)]
            square_ref[pl.ds(place, 2 * ROWS_FULL)] = product(rows, last_ref[...]).astype(BF16)
            return carry

        lax.fori_loop(0, size // (2 * ROWS_FULL), chunk, 0)


def plain_step_kernel(first_step, rows_ref, base_ref, arrived_ref, last_ref, last_t_ref, *refs):
    send_ref = refs[-1]
    scale = rows_ref[1:2] if first_step else rows_ref[2:3]
    odd = position("layer") % 2

    @pl.when(odd == 0)
    def _():
        has_before = (position("layer") > 0).astype(F32)
        term = arrived_ref[...].astype(F32) * (scale * has_before)
        send_ref[...] = (base_ref[...] + term).astype(BF16)

    @pl.when(odd == 1)
    def _():
        block = base_ref[...] + product(arrived_ref[...], last_t_ref[...]) * scale
        send_ref[...] = product(block.astype(BF16), last_ref[...]).astype(BF16)


def step_kernel(first_step, rows_ref, base_ref, arrived_ref, ahead_ref, square_a_ref, square_b_ref, send_ref):
    scale = rows_ref[1:2] if first_step else rows_ref[2:3]
    odd = position("layer") % 2

    @pl.when(odd == 0)
    def _():
        has_before = (position("layer") > 0).astype(F32)
        term = arrived_ref[...].astype(F32) * (scale * has_before)
        send_ref[...] = (base_ref[...] + term).astype(BF16)

    @pl.when(odd == 1)
    def _():
        half = square_a_ref.shape[0]
        term = product(arrived_ref[:, :half], square_a_ref[...])
        term = term + product(arrived_ref[:, half:], square_b_ref[...])
        block = ahead_ref[...] + term * scale
        send_ref[...] = block.astype(BF16)


def row_scales(gram):
    return lax.rsqrt(jnp.sum(gram * identity(gram.shape[0]), axis=1, keepdims=True))


def outer_kernel(count, rows_ref, base_ref, arrived_ref, last_t_ref, next_ref):
    def store(block):
        next_ref[...] = block

    add_arrived(count, rows_ref[2:3], base_ref, arrived_ref, last_t_ref, store)


def scale_kernel(parts, length, *refs):
    grams, (outer_ref, rest_ref, all_ref, all16_ref, low_ref, gram_ref) = refs[:parts], refs[parts:]
    scales = row_scales(sum(ref[...] for ref in grams) * (1.0 / length))
    edge = low_ref.shape[1]
    total = 0.0
    for i in range(all_ref.shape[0]):
        block = (rest_ref[i - 1] if i else outer_ref[...]) * scales
        all_ref[i] = block
        rounded = block.astype(BF16)
        all16_ref[i] = rounded
        low_ref[i] = rounded[:edge]
        total = total + product_t(block, block, HIGHEST)
    gram_ref[...] = total


def first_factor_kernel(parts, length, *refs):
    grams, (scaled_ref, inverse_ref, all_ref) = refs[:parts], refs[parts:]
    gram = sum(ref[...] for ref in grams) * (1.0 / length)
    scales = row_scales(gram)
    across = jnp.sum(identity(gram.shape[0]) * scales, axis=0, keepdims=True)
    inverse_ref[...] = inverse_factors(gram * scales * across)[0]
    for i in range(all_ref.shape[0]):
        all_ref[i] = exact(inverse_ref[...], scaled_ref[i])


def cross_kernel(gram_ref, all16_ref, above_ref, out_ref):
    size, edge = gram_ref.shape[0], above_ref.shape[1]
    places = range(above_ref.shape[0])
    out_ref[:, :size] = gram_ref[...]
    out_ref[:, size : size + edge] = sum(product_t(all16_ref[i], above_ref[i]) for i in places)
    out_ref[:edge, size + edge :] = sum(product_t(above_ref[i], above_ref[i]) for i in places)
    out_ref[edge:, size + edge :] = jnp.zeros((size - edge, edge), F32)


def factor_kernel(parts, length, slices, *refs):
    grams, (first_ref, all_ref, inverse_ref, weights_ref, up_ref) = refs[:parts], refs[parts:]
    size, edge = all_ref.shape[1], up_ref.shape[1]
    first = first_ref[...]
    total = sum(ref[...] for ref in grams) * (1.0 / length)
    has_above = (position("cuts") < slices - 1).astype(F32)
    above = total[:edge, size + edge :] * has_above + identity(edge) * (1.0 - has_above)
    cross = exact(first, total[:, size : size + edge]) * has_above
    own = product_t(exact(first, total[:, :size]), first, HIGHEST)
    inverse, above = inverse_factors(own, above)
    inverse_ref[...] = inverse
    high = inverse[size - edge :]
    correlation = product_t(exact(high, cross), above, HIGHEST)
    up = exact(correlation.T, high)
    for i in range(all_ref.shape[0]):
        up_ref[i] = jnp.dot(up.astype(BF16), all_ref[i].astype(BF16), preferred_element_type=F32).astype(BF16)
    weights_ref[...] = exact(correlation, above)


def by_layer(layers, store):
    for parity in (0, 1):

        @pl.when(position("layer") % 2 == parity)
        def _():
            for place, layer in enumerate(range(layers)[:: -1 if parity else 1]):
                store(layer, place)


def vectors_kernel(inverse_ref, weights_ref, first_ref, above_ref, low_ref, out_ref, block_ref, sem):
    layers, size, _ = first_ref.shape
    edge = low_ref.shape[1]
    blocks = []
    for i in range(layers):
        block = exact(inverse_ref[...], first_ref[i])
        high = block[size - edge :] - exact(weights_ref[...], above_ref[i].astype(F32))
        low_ref[i] = block[:edge]
        blocks.append(jnp.concatenate([block[edge : size - edge], high], 0))

    def store(layer, place):
        block_ref[:, layer, :] = blocks[place]

    by_layer(layers, store)
    copy = pltpu.make_async_copy(block_ref, out_ref.at[pl.ds(edge, size - edge)], sem)
    copy.start()
    copy.wait()


def final_kernel(low_ref, below_ref, _, out_ref, block_ref, sem):
    layers, edge, _ = low_ref.shape
    has_below = (position("cuts") > 0).astype(F32)

    def store(layer, place):
        block_ref[:, layer, :] = low_ref[place] - below_ref[place].astype(F32) * has_below

    by_layer(layers, store)
    copy = pltpu.make_async_copy(block_ref, out_ref.at[pl.ds(0, edge)], sem)
    copy.start()
    copy.wait()


def per_device(vectors, diag_blocks, couplings, bounds):
    vectors = vectors[0]
    count_vec, layers, width = vectors.shape
    count, slices = lax.axis_size("layer"), lax.axis_size("cuts")
    length_all = count * layers * width

    def array(dtype, *shape):
        return jax.ShapeDtypeStruct(shape, dtype)

    outer32, outer16 = array(F32, count_vec, width), array(BF16, count_vec, width)
    rest32, rest16 = array(F32, layers - 1, count_vec, width), array(BF16, layers - 1, count_vec, width)
    square = array(F32, count_vec, count_vec)
    matrix = array(BF16, width, width)
    matrices = array(BF16, 2, layers - 1, width, width)
    edges = array(BF16, layers, EDGE, width)
    one = 2 * count_vec * width * width

    def call(kernel, outs, *operands, far=(), far_out=(), scratch_shapes=(), flops=one, aliases=()):
        moved = sum(x.size * x.dtype.itemsize for x in operands)
        return pl.pallas_call(
            kernel,
            out_shape=outs,
            in_specs=[HBM if i in far else VMEM for i in range(len(operands))],
            out_specs=(
                tuple(HBM if i in far_out else VMEM for i in range(len(outs)))
                if isinstance(outs, tuple)
                else VMEM
            ),
            scratch_shapes=list(scratch_shapes),
            input_output_aliases=dict(aliases),
            compiler_params=pltpu.CompilerParams(vmem_limit_bytes=32 * 2**20),
            cost_estimate=pl.CostEstimate(flops=flops, bytes_accessed=moved, transcendentals=0),
        )(*operands)

    outer, rest, outer_r, rest_r, inner_send, outer_send, last, mids, rows = call(
        enter_kernel,
        (outer32, rest32, outer16, rest16, outer16, outer16, matrix, matrices, array(F32, 8, width)),
        *map(far_away, (bounds, vectors, couplings)), far=(0, 1, 2),
        scratch_shapes=[
            pltpu.SMEM(bounds.shape, jnp.int32),
            pltpu.VMEM(vectors.shape, F32),
            pltpu.SemaphoreType.DMA((4,)),
        ],
    )

    last_t, mids = call(turn_kernel, (matrix, matrices), last, mids, aliases={1: 1})
    half = array(BF16, width // 2, width)
    squares = [call(functools.partial(square_kernel, i), half, last, last_t) for i in range(2)]
    outer_a, outer_b = outer, outer_r
    outer_now, rest_before = outer, rest
    reaches = doublings()
    applications = STEPS * DEG
    for step in range(applications):
        final, gram = step == applications - 1, step == DEG
        ahead = 1 < step < applications - 1
        adds = step > DEG and bool(reaches) and not final
        outer_in = exchanged(outer_send, 1)
        inner_in = exchanged(inner_send, 0)
        base, rest_next, *extra = call(
            functools.partial(interior_kernel, count, layers, step, ahead, gram, adds, final),
            (outer32, rest32)
            + ((outer32,) if step else ())
            + (() if final else (rest16, outer16))
            + ((outer32,) if ahead else ())
            + ((square,) if gram or adds else ()),
            rows, outer_a, outer_b, rest_r, inner_in, diag_blocks, last, last_t, mids,
            rest, outer_now, rest_before,
            *((total, swapped(total, reaches.pop(0))) if adds else ()),
            scratch_shapes=[pltpu.VMEM((count_vec, width), F32)],
            flops=int(2 * (3 * layers - 1) * one),
        )
        if step:
            outer_now = extra.pop(0)
        if gram or adds:
            total = extra[-1]
        if gram and not reaches:
            total = lax.psum(total, "layer")
        if final:
            break
        rest_r, inner_send = extra[:2]
        if ahead:
            outer_send = call(
                functools.partial(step_kernel, step % DEG == 0),
                outer16, rows, base, outer_in, extra[2], *squares,
            )
        else:
            outer_send = call(
                functools.partial(plain_step_kernel, step % DEG == 0),
                outer16, rows, base, outer_in, last, last_t, *squares[:step],
            )
        outer_a, outer_b = base, outer_in
        rest_before, rest = rest, rest_next

    totals = [total]
    for reach in reaches:
        totals = [sum(totals), swapped(sum(totals), reach)]
    outer = call(functools.partial(outer_kernel, count), outer32, rows, base, outer_in, last_t)
    field32 = array(F32, layers, count_vec, width)
    field16 = array(BF16, layers, count_vec, width)
    scaled, scaled_r, low, gram = call(
        functools.partial(scale_kernel, len(totals), length_all),
        (field32, field16, edges, square), *totals, outer, rest_next,
    )
    above = rotated(low, -1)
    cross = call(
        cross_kernel, array(F32, count_vec, count_vec + 2 * EDGE), gram, scaled_r, above
    )
    first, first_all = call(
        functools.partial(first_factor_kernel, len(totals), length_all),
        (square, field32), *totals, scaled,
    )
    grams = partial_sums(cross)
    inverse, weights, up = call(
        functools.partial(factor_kernel, len(grams), length_all, slices),
        (square, array(F32, EDGE, EDGE), edges), *grams, first, first_all,
    )
    below = rotated(up, 1)
    whole = array(F32, count_vec, layers, width)
    low, result = call(
        vectors_kernel, (array(F32, layers, EDGE, width), whole),
        inverse, weights, first_all, above, far_out=(1,),
        scratch_shapes=[
            pltpu.VMEM((count_vec - EDGE, layers, width), F32), pltpu.SemaphoreType.DMA,
        ],
    )
    (result,) = call(
        final_kernel, (whole,), low, below, result, far=(2,), far_out=(0,), aliases={2: 0},
        scratch_shapes=[pltpu.VMEM((EDGE, layers, width), F32), pltpu.SemaphoreType.DMA],
    )
    return result[None]


def solution(mesh):
    in_specs = (
        P("cuts", None, "layer", None),
        P("layer", None, None),
        P("layer", None, None),
        P("cuts", None),
    )
    out_specs = P("cuts", None, "layer", None)
    return jax.shard_map(
        per_device, mesh=mesh, in_specs=in_specs, out_specs=out_specs, check_vma=False
    )
```
